128 devices in a mesh: shell: 8 (over x, z_hi), rank: 16 (over z_lo, y, core).
Axes of the slice: x: 4, y: 4, z: 4 (z_hi: 2, z_lo: 2; z = z_hi * 2 + z_lo), core: 2. Of those that a mesh axis runs over, the one named last changes fastest.
Arguments:
- coefs: float32 [16, 3, 65536], P(None, None, ('shell', 'rank')), may hold values from -3 to 3
- radii: float32 [65536], P(('shell', 'rank')), may hold values from 0.5 to 2
- pair_blocks: int32 [2, 1024], P(None, ('shell', 'rank')), may hold values from 0 to 63, as said below
- pair_count: int32 [128], P(('shell', 'rank')), may hold values from 1 to 8
Outputs:
- intensity: float32 [65536], P(('shell', 'rank'))
The draws below stay inside these ranges and needn't reach their ends.
Inputs may be any that keep to these rules, and one draw needn't show every extreme that they name: pair_blocks[0] is below 32; pair_blocks[1] differs from pair_blocks[0] and is below 32 in slots of the last shell group.
All inputs are finite; a program needn't handle non-finite values.
Results may differ from the reference program's by a relative error of at most 0.0003.
Values sent between devices are 32-bit elements; how exact they have to be, the bound alone decides.
No kernel may reach another device: no remote copies, remote signals or barrier semaphores. Data moves between devices by JAX's collectives and lax.ppermute only.
A program may use at most 64 MiB of HBM per device.

```python
import math
import jax
import jax.numpy as jnp
from jax import lax

NCOEF = 16
TIMES = 64
BLOCK = 256
PAIRS_DEV = 8
SHELLS = 8
RANKS = 16
BLK_SHELL = 32
OBJECTS = 65536
PAIR_SLOTS = 1024
DEVICES = 128


def draw_pair_blocks(key, part):
    key = jax.random.fold_in(key, 11)
    keys = jax.random.split(key, 5)
    index = jnp.arange(PAIR_SLOTS, dtype=jnp.int32)
    group = index // (RANKS * PAIRS_DEV)
    first = jax.random.randint(keys[0], (PAIR_SLOTS,), 0, BLK_SHELL)
    other = (first + 1 + jax.random.randint(keys[1], (PAIR_SLOTS,), 0, BLK_SHELL - 1)) % BLK_SHELL
    across = jax.random.randint(keys[2], (PAIR_SLOTS,), 0, BLK_SHELL)
    upward = (jax.random.randint(keys[3], (PAIR_SLOTS,), 0, 2) == 1) & (group < SHELLS - 1)
    second = jnp.where(upward, BLK_SHELL + across, other)
    half = RANKS * PAIRS_DEV // 2
    picks = jax.random.randint(keys[4], (2,), 0, half)
    first = jnp.where(index == picks[0], 0, first)
    second = jnp.where(index == picks[0], 2 * BLK_SHELL - 1, second)
    first = jnp.where(index == half + picks[1], BLK_SHELL - 1, first)
    second = jnp.where(index == half + picks[1], 0, second)
    return jnp.stack([first, second]).astype(jnp.int32)


def draw_pair_count(key, part):
    key = jax.random.fold_in(key, 23)
    keys = jax.random.split(key, 2)
    count = jax.random.randint(keys[0], (DEVICES,), 1, PAIRS_DEV + 1)
    pick = jax.random.randint(keys[1], (), 0, DEVICES)
    return jnp.where(jnp.arange(DEVICES) == pick, PAIRS_DEV, count).astype(jnp.int32)


def block_levels(key, extent, pieces, least, largest):
    loudness = 1.0
    for axis_at, blocks in pieces:
        steps = jax.random.uniform(jax.random.fold_in(jax.random.fold_in(key, 6), axis_at), (blocks,), jnp.float32, least / len(pieces), largest / len(pieces))
        loudness = loudness * jnp.repeat(jnp.exp(steps), extent[axis_at] // blocks).reshape((-1,) + (1,) * (len(extent) - 1 - axis_at))
    return loudness


def centred(stream_key, dims, spread, most, shards=(), held_as=jnp.bfloat16):
    drawn = jax.random.normal(stream_key, dims, jnp.float32) * spread
    if len(shards) > 0:
        drawn = block_levels(stream_key, dims, shards, -0.22, 0.18) * drawn
    return jnp.clip(drawn, min=-most, max=most).astype(held_as)


def setup_inputs(seed: int = 0) -> dict:
    seeds = jax.random.split(jax.random.key(seed), 5)
    coefs = centred(seeds[0], (NCOEF, 3, OBJECTS), 0.5, 3.0, ((2, 128),), jnp.float32)
    radii = jnp.clip(jnp.exp(math.log(2.0) - 1.3862944 * jax.random.uniform(seeds[1], (OBJECTS,), jnp.float32) ** block_levels(seeds[1], (OBJECTS,), ((0, 128),), -0.2, 0.2)), 0.5, 2.0)
    pair_blocks = draw_pair_blocks(jax.random.fold_in(seeds[4], 71), 0)
    pair_count = draw_pair_count(jax.random.fold_in(seeds[4], 71), 0)
    return {"coefs": coefs, "radii": radii, "pair_blocks": pair_blocks, "pair_count": pair_count}


def cheb_table(ncoef, times):
    node = -1.0 + (2.0 * jnp.arange(times, dtype=jnp.float32) + 1.0) / times
    order = jnp.arange(ncoef, dtype=jnp.float32)
    return jnp.cos(order[None, :] * jnp.arccos(node)[:, None])


def evaluate(table, coefs):
    flat = coefs.reshape(coefs.shape[0], -1)
    values = jnp.dot(table, flat, precision=lax.Precision.HIGHEST, preferred_element_type=jnp.float32)
    return values.reshape(table.shape[0], coefs.shape[1], coefs.shape[2])


def pair_terms(first_pos, second_pos, first_rad, second_rad):
    diff_x = first_pos[:, 0, :, None] - second_pos[:, 0, None, :]
    diff_y = first_pos[:, 1, :, None] - second_pos[:, 1, None, :]
    diff_z = first_pos[:, 2, :, None] - second_pos[:, 2, None, :]
    gap = diff_x * diff_x + diff_y * diff_y + diff_z * diff_z
    summed = first_rad[:, None] + second_rad[None, :]
    reach = summed * summed
    weight = reach[None, :, :] / (reach[None, :, :] + gap)
    factor = 1.0 / (first_pos.shape[0] * first_pos.shape[2])
    return jnp.sum(weight, axis=(0, 2)) * factor, jnp.sum(weight, axis=(0, 1)) * factor


def reference(coefs, radii, pair_blocks, pair_count):
    table = cheb_table(NCOEF, TIMES)
    positions = evaluate(table, coefs)

    def step(total, index):
        device = index // PAIRS_DEV
        group = device // RANKS
        live = (index % PAIRS_DEV) < pair_count[device]
        base = group * BLK_SHELL
        first = ((base + pair_blocks[0, index]) * BLOCK).astype(jnp.int32)
        second = ((base + pair_blocks[1, index]) * BLOCK).astype(jnp.int32)

        def credit(total):
            row, col = pair_terms(lax.dynamic_slice_in_dim(positions, first, BLOCK, 2),
                                  lax.dynamic_slice_in_dim(positions, second, BLOCK, 2),
                                  lax.dynamic_slice_in_dim(radii, first, BLOCK, 0),
                                  lax.dynamic_slice_in_dim(radii, second, BLOCK, 0))
            total = lax.dynamic_update_slice_in_dim(total, lax.dynamic_slice_in_dim(total, first, BLOCK, 0) + row, first, 0)
            total = lax.dynamic_update_slice_in_dim(total, lax.dynamic_slice_in_dim(total, second, BLOCK, 0) + col, second, 0)
            return total

        return lax.cond(live, credit, lambda kept: kept, total), None

    total, unused = lax.scan(step, jnp.zeros((OBJECTS,), jnp.float32), jnp.arange(PAIR_SLOTS, dtype=jnp.int32))
    return total
```

```python
import jax
import jax.numpy as jnp
import numpy as np
from jax import lax
from jax.experimental import pallas as pl
from jax.experimental.pallas import tpu as pltpu
from jax.sharding import PartitionSpec as P

NCOEF = 16
TIMES = 64
BLOCK = 256
RANKS = 16
SLOTS = 8
BLOCKS = 32
SPAN = BLOCKS * BLOCK
HELD = 512
UNROLL = 8
LIST = RANKS * SLOTS + UNROLL
TILE = 64
F32 = jnp.float32
BF16 = jnp.bfloat16
VMEM = pltpu.VMEM
SMEM = pltpu.SMEM
PARAMS = pltpu.CompilerParams(vmem_limit_bytes=56 * 1024 * 1024)


def passed_along(value, axis, steps):
    count = lax.axis_size(axis)
    leading, last = (max(0, -steps), min(count, count - steps))
    return lax.ppermute(value, axis, [(source, source + steps) for source in range(leading, last)])


def spread_table():
    node = -1.0 + (2.0 * np.arange(TIMES) + 1.0) / TIMES
    table = np.cos(np.arange(NCOEF)[None, :] * np.arccos(node)[:, None])
    spread = np.zeros((TIMES, 4, 3, NCOEF), np.float32)
    for c in range(3):
        spread[:, c, c, :] = table
    return spread.reshape(TIMES * 4, 3 * NCOEF)


def evaluate_kernel(pairs, count, table, coefs, radii, out):
    flat = jnp.concatenate([coefs[:, c, :] for c in range(3)], axis=0)
    values = jnp.dot(table[...], flat, precision=lax.Precision.HIGHEST, preferred_element_type=F32)
    lane = lax.broadcasted_iota(jnp.int32, (1, HELD), 1)
    info = jnp.where(lane == 2 * SLOTS, count[0].astype(F32), 0.0)
    for side in range(2):
        for slot in range(SLOTS):
            info = jnp.where(lane == side * SLOTS + slot, pairs[side, slot].astype(F32), info)
    row = lax.broadcasted_iota(jnp.int32, (16, HELD), 0)
    extra = jnp.where(row == 3, radii[...].reshape(1, HELD), jnp.where(row == 7, info, 0.0))
    out[...] = values.reshape(RANKS, 16, HELD) + extra[None]


def pieces(x):
    high = x.astype(BF16)
    rest = x - high.astype(F32)
    mid = rest.astype(BF16)
    low = (rest - mid.astype(F32)).astype(BF16)
    return high, mid, low


def features(slab):
    n = slab.shape[1]
    part = lax.broadcasted_iota(jnp.int32, (16, n), 0) % 4
    values = jnp.where(part == 3, jnp.broadcast_to(slab[3:4, :], (16, n)), slab)
    square = (values * values).reshape(2, 8, n)
    row = lax.broadcasted_iota(jnp.int32, (2, 8, n), 1)
    twos = square + jnp.where(row % 2 == 1, pltpu.roll(square, 1, 1), pltpu.roll(square, 7, 1))
    fours = twos + jnp.where((row // 2) % 2 == 1, pltpu.roll(twos, 2, 1), pltpu.roll(twos, 6, 1))
    high, mid, low = pieces(values)
    s_high, s_mid, s_low = (p.astype(F32) for p in pieces(fours.reshape(16, n)))
    zero = jnp.zeros((16, n), F32)
    sums = jnp.where(part == 0, s_high, jnp.where(part == 1, s_mid, jnp.where(part == 2, s_low, zero)))
    ones = jnp.where(part == 3, zero, 1.0)
    return high, mid, low, sums, ones, part


def prepare_second(second, second_radii, received, rank):
    slab = received[rank]
    high, mid, low, sums, ones, _ = features(slab)
    terms = (high, mid, high, low, high, mid, sums.astype(BF16), ones.astype(BF16))
    for i, term in enumerate(terms):
        second[16 * i : 16 * i + 16, rank * HELD : (rank + 1) * HELD] = term
    for half in range(HELD // BLOCK):
        block = rank * (HELD // BLOCK) + half
        second_radii[block : block + 1, :] = slab[3:4, half * BLOCK : (half + 1) * BLOCK]


def prepare_first(first, first_radii, received, rank):
    slab = received[rank]
    high, mid, low, sums, ones, part = features(slab)
    scale = jnp.where(part == 3, 2.0, -2.0)
    high, mid, low = (scale * p.astype(F32) for p in (high, mid, low))
    terms = jnp.concatenate([high, high, mid, high, low, mid, ones, sums], axis=0)
    for c in range(0, HELD, 128):
        at = rank * HELD + c
        first[at : at + 128, :] = terms[:, c : c + 128].T.astype(BF16)
        first_radii[at : at + 128, :] = jnp.broadcast_to(slab[3:4, c : c + 128], (128, 128)).T


def credit_pair(first, first_radii, second, second_radii, rows, columns, a, b):
    from_a = pl.multiple_of(lax.rem(a, BLOCKS) * BLOCK, BLOCK)
    block_b = lax.rem(b, BLOCKS)
    of_b = second[:, pl.ds(pl.multiple_of(block_b * BLOCK, BLOCK), BLOCK)]
    radii_b = second_radii[pl.ds(block_b, 1), :]
    lane = lax.broadcasted_iota(jnp.int32, (TILE, 128), 1)
    masks = [jnp.where((lane % 16) // 4 == t, 1.0, 0.0).astype(BF16) for t in range(4)]
    column = jnp.zeros((8, BLOCK), F32)
    for i in range(0, BLOCK, TILE):
        of_a = first[pl.ds(from_a + i, TILE), :]
        total = None
        for mask in masks:
            whole = jnp.dot(of_a * mask, of_b, preferred_element_type=F32)
            inverse = pl.reciprocal(whole, approx=False)
            total = inverse if total is None else total + inverse
        radii_a = first_radii[pl.ds(from_a + i, TILE), :]
        summed = jnp.concatenate([radii_a, radii_a], axis=1) + radii_b
        weight = total * (summed * summed)
        column = column + jnp.sum(weight.reshape(TILE // 8, 8, BLOCK), axis=0)
        row = jnp.sum(weight[:, :128] + weight[:, 128:], axis=1, keepdims=True)
        rows[i : i + TILE, :] = rows[i : i + TILE, :] + jnp.where(lane == a, row, 0.0)
    at = pl.ds(pl.multiple_of(b * 8, 8), 8)
    columns[at, :] = columns[at, :] + column


def credit_list(first, first_radii, second, second_radii, rows, columns, pairs, count):
    rows[...] = jnp.zeros_like(rows)
    columns[...] = jnp.zeros_like(columns)

    @pl.loop(0, (count + UNROLL - 1) // UNROLL)
    def _(step):
        for u in range(UNROLL):
            at = step * UNROLL + u
            credit_pair(first, first_radii, second, second_radii, rows, columns, pairs[0, at], pairs[1, at])


def block_sums(columns):
    return jnp.sum(columns[0 : 8 * BLOCKS, :].reshape(BLOCKS, 8, BLOCK), axis=1)


def own_kernel(
    received, credited, first, first_radii, crossing,
    second, second_radii, rows, columns, info, lists, own, sem,
):
    info[...] = received[:, 7, 0:128].astype(jnp.int32)
    copy = pltpu.make_async_copy(info, lists, sem)
    copy.start()
    for rank in range(RANKS):
        prepare_second(second, second_radii, received, rank)
        prepare_first(first, first_radii, received, rank)
    copy.wait()

    def gather(device, counts):
        def slot(k, counts):
            a, b = lists[device, k], lists[device, SLOTS + k]
            n_own, n_cross = counts
            crosses = b >= BLOCKS
            own[0, n_own] = a
            own[1, n_own] = b
            crossing[0, n_cross] = a
            crossing[1, n_cross] = b - BLOCKS
            return (n_own + jnp.where(crosses, 0, 1), n_cross + jnp.where(crosses, 1, 0))

        return lax.fori_loop(0, lists[device, 2 * SLOTS], slot, counts)

    n_own, n_cross = lax.fori_loop(0, RANKS, gather, (jnp.int32(0), jnp.int32(0)))
    for u in range(UNROLL):
        for side in range(2):
            own[side, n_own + u] = BLOCKS
            crossing[side, n_cross + u] = BLOCKS
    crossing[2, 0] = n_cross
    credit_list(first, first_radii, second, second_radii, rows, columns, own, n_own)
    credited[...] = rows[...].T[0:BLOCKS, :] + block_sums(columns)


def cross_kernel(
    crossing, received, earlier, first_hbm, first_radii_hbm, out,
    first, first_radii, second, second_radii, rows, columns, sem,
):
    copies = [
        pltpu.make_async_copy(first_hbm, first, sem.at[0]),
        pltpu.make_async_copy(first_radii_hbm, first_radii, sem.at[1]),
    ]
    for copy in copies:
        copy.start()
    for rank in range(RANKS):
        prepare_second(second, second_radii, received, rank)
    for copy in copies:
        copy.wait()
    credit_list(first, first_radii, second, second_radii, rows, columns, crossing, crossing[2, 0])
    factor = 1.0 / (TIMES * BLOCK)
    own = (earlier[...] + rows[...].T[0:BLOCKS, :]) * factor
    beyond = block_sums(columns) * factor
    for block in range(BLOCKS):
        rank, half = divmod(block, 2)
        for k in range(2):
            at = 2 * half + k
            out[rank, at : at + 1, :] = own[block : block + 1, k * 128 : (k + 1) * 128]
            out[rank, 4 + at : 5 + at, :] = beyond[block : block + 1, k * 128 : (k + 1) * 128]


def body(coefs, radii, pair_blocks, pair_count):
    in_vmem, in_smem = pl.BlockSpec(memory_space=VMEM), pl.BlockSpec(memory_space=SMEM)
    anywhere = pl.BlockSpec(memory_space=pl.ANY)
    at_all = pl.pallas_call(
        evaluate_kernel,
        out_shape=jax.ShapeDtypeStruct((RANKS, 16, HELD), F32),
        in_specs=[in_smem, in_smem, in_vmem, in_vmem, in_vmem],
        out_specs=in_vmem,
        compiler_params=PARAMS,
        name="evaluate",
    )(pair_blocks, pair_count, jnp.asarray(spread_table()), coefs, radii)
    received = lax.all_to_all(at_all, "rank", 0, 0)
    beyond = passed_along(received, "shell", -1)
    credited, first, first_radii, crossing = pl.pallas_call(
        own_kernel,
        out_shape=[
            jax.ShapeDtypeStruct((BLOCKS, BLOCK), F32),
            jax.ShapeDtypeStruct((SPAN, 128), BF16),
            jax.ShapeDtypeStruct((SPAN, 128), F32),
            jax.ShapeDtypeStruct((3, LIST), jnp.int32),
        ],
        in_specs=[in_vmem],
        out_specs=[in_vmem, in_vmem, in_vmem, in_smem],
        scratch_shapes=[
            VMEM((128, SPAN), BF16),
            VMEM((BLOCKS, BLOCK), F32),
            VMEM((BLOCK, 128), F32),
            VMEM((8 * BLOCKS + 8, BLOCK), F32),
            VMEM((RANKS, 128), jnp.int32),
            SMEM((RANKS, 128), jnp.int32),
            SMEM((2, LIST), jnp.int32),
            pltpu.SemaphoreType.DMA,
        ],
        compiler_params=PARAMS,
        cost_estimate=pl.CostEstimate(flops=8_000_000_000, bytes_accessed=8_000_000, transcendentals=0),
        name="own_pairs",
    )(received)
    partial = pl.pallas_call(
        cross_kernel,
        out_shape=jax.ShapeDtypeStruct((RANKS, 8, 128), F32),
        in_specs=[in_smem, in_vmem, in_vmem, anywhere, anywhere],
        out_specs=in_vmem,
        scratch_shapes=[
            VMEM((SPAN, 128), BF16),
            VMEM((SPAN, 128), F32),
            VMEM((128, SPAN), BF16),
            VMEM((BLOCKS, BLOCK), F32),
            VMEM((BLOCK, 128), F32),
            VMEM((8 * BLOCKS + 8, BLOCK), F32),
            pltpu.SemaphoreType.DMA((2,)),
        ],
        compiler_params=PARAMS,
        cost_estimate=pl.CostEstimate(flops=8_000_000_000, bytes_accessed=8_000_000, transcendentals=0),
        name="crossing_pairs",
    )(crossing, beyond, credited, first, first_radii)
    summed = jnp.sum(lax.all_to_all(partial, "rank", 0, 0), axis=0)
    returned = passed_along(summed[4:], "shell", 1)
    return (summed[:4] + returned).reshape(HELD)


def solution(mesh):
    placed = (
        P(None, None, ("shell", "rank")),
        P(("shell", "rank")),
        P(None, ("shell", "rank")),
        P(("shell", "rank")),
    )
    return jax.shard_map(
        body, mesh=mesh, in_specs=placed, out_specs=P(("shell", "rank")), check_vma=False
    )
```

```python
import jax
import jax.numpy as jnp
import numpy as np
from jax import lax
from jax.experimental import pallas as pl
from jax.experimental.pallas import tpu as pltpu
from jax.sharding import PartitionSpec as P

NCOEF = 16
TIMES = 64
BLOCK = 256
RANKS = 16
SLOTS = 8
BLOCKS = 32
SPAN = BLOCKS * BLOCK
HELD = 512
UNROLL = 8
LIST = 160
LISTS = 512
COUNTS = 480
TILE = 64
F32 = jnp.float32
BF16 = jnp.bfloat16
VMEM = pltpu.VMEM
SMEM = pltpu.SMEM
PARAMS = pltpu.CompilerParams(vmem_limit_bytes=24 * 1024 * 1024)


def passed_along(value, axis, steps):
    count = lax.axis_size(axis)
    leading, last = (max(0, -steps), min(count, count - steps))
    return lax.ppermute(value, axis, [(source, source + steps) for source in range(leading, last)])


def spread_table():
    node = -1.0 + (2.0 * np.arange(TIMES) + 1.0) / TIMES
    table = np.cos(np.arange(NCOEF)[None, :] * np.arccos(node)[:, None])
    spread = np.zeros((TIMES, 4, 3, NCOEF), np.float32)
    for c in range(3):
        spread[:, c, c, :] = table
    return spread.reshape(TIMES * 4, 3 * NCOEF)


def evaluate_kernel(pairs, count, table, coefs, radii, out):
    values = jnp.dot(
        table[...], coefs[...].reshape(3 * NCOEF, HELD), precision=lax.Precision.HIGHEST, preferred_element_type=F32
    )
    lane = lax.broadcasted_iota(jnp.int32, (1, HELD), 1)
    sides = []
    for side in range(2):
        blocks = jnp.zeros((1, HELD), F32)
        for slot in range(SLOTS):
            blocks = jnp.where(lane == slot, pairs[side, slot].astype(F32), blocks)
        sides.append(blocks)
    row = lax.broadcasted_iota(jnp.int32, (16, HELD), 0)
    extra = jnp.where(row == 15, count[0].astype(F32), 0.0)
    for at, line in ((3, radii[...].reshape(1, HELD)), (7, sides[0]), (11, sides[1])):
        extra = jnp.where(row == at, line, extra)
    out[...] = values.reshape(RANKS, 16, HELD) + extra[None]


def list_pairs(received):
    first, second, count = (received[:, row, 0:128] for row in (7, 11, 15))
    lane = lax.broadcasted_iota(jnp.int32, (RANKS, 128), 1)
    live = (lane < SLOTS) & (lane.astype(F32) < count)
    before_lane = jnp.where(
        lax.broadcasted_iota(jnp.int32, (128, 128), 0) < lax.broadcasted_iota(jnp.int32, (128, 128), 1), 1.0, 0.0
    ).astype(BF16)
    before_rank = jnp.where(
        lax.broadcasted_iota(jnp.int32, (RANKS, RANKS), 1) < lax.broadcasted_iota(jnp.int32, (RANKS, RANKS), 0), 1.0, 0.0
    ).astype(BF16)
    ones = jnp.ones((128, 128), BF16)
    crosses = second >= BLOCKS
    place = jnp.full((RANKS, 128), -1.0, F32)
    totals = []
    for which, chosen in enumerate((live & ~crosses, live & crosses)):
        flag = jnp.where(chosen, 1.0, 0.0).astype(BF16)
        within = jnp.dot(flag, before_lane, preferred_element_type=F32)
        ranks = jnp.dot(before_rank, flag, preferred_element_type=F32).astype(BF16)
        position = within + jnp.dot(ranks, ones, preferred_element_type=F32)
        place = jnp.where(chosen, position + which * LIST, place)
        totals.append(jnp.sum(flag.astype(F32), keepdims=True))
    second = jnp.where(crosses, second - BLOCKS, second)
    target = lax.broadcasted_iota(jnp.int32, (RANKS, LISTS), 1).astype(F32)
    sides = [jnp.zeros((RANKS, LISTS), F32)] * 2
    for slot in range(SLOTS):
        hit = place[:, slot : slot + 1] == target
        sides = [
            kept + jnp.where(hit, side[:, slot : slot + 1] - BLOCKS, 0.0) for kept, side in zip(sides, (first, second))
        ]
    lists = jnp.concatenate([jnp.sum(side, axis=0, keepdims=True) for side in sides], axis=0) + BLOCKS
    for which, total in enumerate(totals):
        lists = jnp.where(target[0:2] == COUNTS + which, total, lists)
    return lists.astype(jnp.int32)


def pieces(x):
    high = x.astype(BF16)
    rest = x - high.astype(F32)
    mid = rest.astype(BF16)
    low = (rest - mid.astype(F32)).astype(BF16)
    return high, mid, low


def features(slab):
    n = slab.shape[1]
    part = lax.broadcasted_iota(jnp.int32, (16, n), 0) % 4
    values = jnp.where(part == 3, jnp.broadcast_to(slab[3:4, :], (16, n)), slab)
    square = (values * values).reshape(2, 8, n)
    row = lax.broadcasted_iota(jnp.int32, (2, 8, n), 1)
    twos = square + jnp.where(row % 2 == 1, pltpu.roll(square, 1, 1), pltpu.roll(square, 7, 1))
    fours = twos + jnp.where((row // 2) % 2 == 1, pltpu.roll(twos, 2, 1), pltpu.roll(twos, 6, 1))
    high, mid, low = pieces(values)
    s_high, s_mid, s_low = (p.astype(F32) for p in pieces(fours.reshape(16, n)))
    zero = jnp.zeros((16, n), F32)
    sums = jnp.where(part == 0, s_high, jnp.where(part == 1, s_mid, jnp.where(part == 2, s_low, zero)))
    ones = jnp.where(part == 3, zero, 1.0)
    return high, mid, low, sums, ones, part


def prepare_second(second, second_radii, received, rank):
    slab = received[rank]
    high, mid, low, sums, ones, _ = features(slab)
    terms = (high, mid, high, low, high, mid, sums.astype(BF16), ones.astype(BF16))
    for i, term in enumerate(terms):
        second[16 * i : 16 * i + 16, rank * HELD : (rank + 1) * HELD] = term
    for half in range(HELD // BLOCK):
        block = rank * (HELD // BLOCK) + half
        second_radii[block : block + 1, :] = slab[3:4, half * BLOCK : (half + 1) * BLOCK]


def prepare_first(first, first_radii, received, rank):
    slab = received[rank]
    high, mid, low, sums, ones, part = features(slab)
    scale = jnp.where(part == 3, 2.0, -2.0)
    high, mid, low = (scale * p.astype(F32) for p in (high, mid, low))
    terms = jnp.concatenate([high, high, mid, high, low, mid, ones, sums], axis=0)
    for c in range(0, HELD, 128):
        at = rank * HELD + c
        first[at : at + 128, :] = terms[:, c : c + 128].T.astype(BF16)
        first_radii[at : at + 128, :] = jnp.broadcast_to(slab[3:4, c : c + 128], (128, 128)).T


def credit_pair(first, first_radii, second, second_radii, rows, columns, a, b):
    from_a = pl.multiple_of(lax.rem(a, BLOCKS) * BLOCK, BLOCK)
    block_b = lax.rem(b, BLOCKS)
    of_b = second[:, pl.ds(pl.multiple_of(block_b * BLOCK, BLOCK), BLOCK)]
    radii_b = second_radii[pl.ds(block_b, 1), :]
    lane = lax.broadcasted_iota(jnp.int32, (TILE, 128), 1)
    masks = [jnp.where((lane % 16) // 4 == t, 1.0, 0.0).astype(BF16) for t in range(4)]
    column = jnp.zeros((8, BLOCK), F32)
    for i in range(0, BLOCK, TILE):
        of_a = first[pl.ds(from_a + i, TILE), :]
        total = None
        for mask in masks:
            whole = jnp.dot(of_a * mask, of_b, preferred_element_type=F32)
            inverse = pl.reciprocal(whole, approx=False)
            total = inverse if total is None else total + inverse
        radii_a = first_radii[pl.ds(from_a + i, TILE), :]
        summed = jnp.concatenate([radii_a, radii_a], axis=1) + radii_b
        weight = total * (summed * summed)
        column = column + jnp.sum(weight.reshape(TILE // 8, 8, BLOCK), axis=0)
        row = jnp.sum(weight[:, :128] + weight[:, 128:], axis=1, keepdims=True)
        rows[i : i + TILE, :] = rows[i : i + TILE, :] + jnp.where(lane == a, row, 0.0)
    at = pl.ds(pl.multiple_of(b * 8, 8), 8)
    columns[at, :] = columns[at, :] + column


def credit_list(first, first_radii, second, second_radii, rows, columns, lists, which):
    @pl.loop(0, (lists[0, COUNTS + which] + UNROLL - 1) // UNROLL)
    def _(step):
        for u in range(UNROLL):
            at = which * LIST + step * UNROLL + u
            credit_pair(first, first_radii, second, second_radii, rows, columns, lists[0, at], lists[1, at])


def block_sums(columns):
    return jnp.sum(columns[0 : 8 * BLOCKS, :].reshape(BLOCKS, 8, BLOCK), axis=1)


def own_kernel(
    received, rows, credited, first, first_radii, lists,
    second, second_radii, columns, listed, sem,
):
    lists[...] = list_pairs(received)
    copy = pltpu.make_async_copy(lists, listed, sem)
    copy.start()
    rows[...] = jnp.zeros_like(rows)
    columns[...] = jnp.zeros_like(columns)
    for rank in range(RANKS):
        prepare_second(second, second_radii, received, rank)
        prepare_first(first, first_radii, received, rank)
    copy.wait()
    credit_list(first, first_radii, second, second_radii, rows, columns, listed, 0)
    credited[...] = block_sums(columns)


def cross_kernel(
    lists, received, earlier_rows, earlier, first, first_radii, out,
    second, second_radii, rows, columns,
):
    rows[...] = earlier_rows[...]
    columns[...] = jnp.zeros_like(columns)
    for rank in range(RANKS):
        prepare_second(second, second_radii, received, rank)
    credit_list(first, first_radii, second, second_radii, rows, columns, lists, 1)
    factor = 1.0 / (TIMES * BLOCK)
    own = (earlier[...] + rows[...].T[0:BLOCKS, :]) * factor
    beyond = block_sums(columns) * factor
    for block in range(BLOCKS):
        rank, half = divmod(block, 2)
        for k in range(2):
            at = 2 * half + k
            out[rank, at : at + 1, :] = own[block : block + 1, k * 128 : (k + 1) * 128]
            out[rank, 4 + at : 5 + at, :] = beyond[block : block + 1, k * 128 : (k + 1) * 128]


def body(coefs, radii, pair_blocks, pair_count):
    in_vmem, in_smem = pl.BlockSpec(memory_space=VMEM), pl.BlockSpec(memory_space=SMEM)
    at_all = pl.pallas_call(
        evaluate_kernel,
        out_shape=jax.ShapeDtypeStruct((RANKS, 16, HELD), F32),
        in_specs=[in_smem, in_smem, in_vmem, in_vmem, in_vmem],
        out_specs=in_vmem,
        compiler_params=PARAMS,
        name="evaluate",
    )(pair_blocks, pair_count, jnp.asarray(spread_table()), coefs.transpose(1, 0, 2), radii)
    received = lax.all_to_all(at_all, "rank", 0, 0)
    beyond = passed_along(received, "shell", -1)
    rows, credited, first, first_radii, lists = pl.pallas_call(
        own_kernel,
        out_shape=[
            jax.ShapeDtypeStruct((BLOCK, 128), F32),
            jax.ShapeDtypeStruct((BLOCKS, BLOCK), F32),
            jax.ShapeDtypeStruct((SPAN, 128), BF16),
            jax.ShapeDtypeStruct((SPAN, 128), F32),
            jax.ShapeDtypeStruct((2, LISTS), jnp.int32),
        ],
        in_specs=[in_vmem],
        out_specs=[in_vmem] * 5,
        scratch_shapes=[
            VMEM((128, SPAN), BF16),
            VMEM((BLOCKS, BLOCK), F32),
            VMEM((8 * BLOCKS + 8, BLOCK), F32),
            SMEM((2, LISTS), jnp.int32),
            pltpu.SemaphoreType.DMA,
        ],
        compiler_params=PARAMS,
        cost_estimate=pl.CostEstimate(flops=8_000_000_000, bytes_accessed=8_000_000, transcendentals=0),
        name="own_pairs",
    )(received)
    partial = pl.pallas_call(
        cross_kernel,
        out_shape=jax.ShapeDtypeStruct((RANKS, 8, 128), F32),
        in_specs=[in_smem] + [in_vmem] * 5,
        out_specs=in_vmem,
        scratch_shapes=[
            VMEM((128, SPAN), BF16),
            VMEM((BLOCKS, BLOCK), F32),
            VMEM((BLOCK, 128), F32),
            VMEM((8 * BLOCKS + 8, BLOCK), F32),
        ],
        compiler_params=PARAMS,
        cost_estimate=pl.CostEstimate(flops=8_000_000_000, bytes_accessed=8_000_000, transcendentals=0),
        name="crossing_pairs",
    )(lists, beyond, rows, credited, first, first_radii)
    summed = jnp.sum(lax.all_to_all(partial, "rank", 0, 0), axis=0)
    returned = passed_along(summed[4:], "shell", 1)
    return (summed[:4] + returned).reshape(HELD)


def solution(mesh):
    placed = (
        P(None, None, ("shell", "rank")),
        P(("shell", "rank")),
        P(None, ("shell", "rank")),
        P(("shell", "rank")),
    )
    return jax.shard_map(
        body, mesh=mesh, in_specs=placed, out_specs=P(("shell", "rank")), check_vma=False
    )
```

```python
import jax
import jax.numpy as jnp
import numpy as np
from jax import lax
from jax.experimental import pallas as pl
from jax.experimental.pallas import tpu as pltpu
from jax.sharding import PartitionSpec as P

NCOEF = 16
TIMES = 64
BLOCK = 256
RANKS = 16
SLOTS = 8
BLOCKS = 32
SPAN = BLOCKS * BLOCK
HELD = 512
UNROLL = 8
LIST = 160
LISTS = 512
COUNTS = 480
TILE = 64
F32 = jnp.float32
BF16 = jnp.bfloat16
VMEM = pltpu.VMEM
SMEM = pltpu.SMEM
PARAMS = pltpu.CompilerParams(vmem_limit_bytes=24 * 1024 * 1024)


def passed_along(value, axis, steps):
    count = lax.axis_size(axis)
    leading, last = (max(0, -steps), min(count, count - steps))
    return lax.ppermute(value, axis, [(source, source + steps) for source in range(leading, last)])


EIGHT = ((0, 0), (0, 1), (0, 2), (3, 0), (1, 0), (1, 1), (1, 2), (3, 1))
FOUR = ((2, 0), (2, 1), (2, 2), (3, 2))
CHUNK = 56


def spread_table():
    node = -1.0 + (2.0 * np.arange(TIMES) + 1.0) / TIMES
    table = np.cos(np.arange(NCOEF)[None, :] * np.arccos(node)[:, None])
    spread = np.zeros((RANKS, 16, 3, NCOEF), np.float32)
    for row, (time, coordinate) in enumerate(EIGHT + FOUR + FOUR):
        spread[:, row, coordinate, :] = table[time :: TIMES // RANKS]
    return spread.reshape(RANKS * 16, 3 * NCOEF)


def evaluate_kernel(*refs):
    given, (out, *held, sems) = refs[:5], refs[5:]
    copies = [pltpu.make_async_copy(given[i], held[i], sems.at[i]) for i in range(5)]
    for copy in copies:
        copy.start()
    for copy in copies:
        copy.wait()
    pairs, count, table, coefs, radii = held
    values = jnp.dot(
        table[...], coefs[...].reshape(3 * NCOEF, HELD), precision=lax.Precision.HIGHEST, preferred_element_type=F32
    ).reshape(RANKS, 16, HELD)
    lane = lax.broadcasted_iota(jnp.int32, (1, 128), 1)
    row = lax.broadcasted_iota(jnp.int32, (8, 128), 0)
    last = jnp.where(row == 6, count[0].astype(F32), 0.0)
    for q in range(4):
        last = jnp.where(row == q, radii[128 * q : 128 * q + 128].reshape(1, 128), last)
    for side in range(2):
        blocks = jnp.zeros((1, 128), F32)
        for slot in range(SLOTS):
            blocks = jnp.where(lane == slot, pairs[side, slot].astype(F32), blocks)
        last = jnp.where(row == 4 + side, blocks, last)
    runs = [values[:, :, 128 * q : 128 * q + 128] for q in range(4)]
    for q in range(4):
        out[:, 8 * q : 8 * q + 8, :] = runs[q][:, 0:8]
    for half in range(2):
        out[:, 32 + 8 * half : 40 + 8 * half, :] = jnp.where(
            row[None] < 4, runs[2 * half][:, 8:16], runs[2 * half + 1][:, 8:16]
        )
    out[:, 48:56, :] = jnp.broadcast_to(last[None], (RANKS, 8, 128))


def list_pairs(received):
    first, second, count = (received[:, row, 0:128] for row in (52, 53, 54))
    lane = lax.broadcasted_iota(jnp.int32, (RANKS, 128), 1)
    live = (lane < SLOTS) & (lane.astype(F32) < count)
    before_lane = jnp.where(
        lax.broadcasted_iota(jnp.int32, (128, 128), 0) < lax.broadcasted_iota(jnp.int32, (128, 128), 1), 1.0, 0.0
    ).astype(BF16)
    before_rank = jnp.where(
        lax.broadcasted_iota(jnp.int32, (RANKS, RANKS), 1) < lax.broadcasted_iota(jnp.int32, (RANKS, RANKS), 0), 1.0, 0.0
    ).astype(BF16)
    ones = jnp.ones((128, 128), BF16)
    crosses = second >= BLOCKS
    place = jnp.full((RANKS, 128), -1.0, F32)
    totals = []
    for which, chosen in enumerate((live & ~crosses, live & crosses)):
        flag = jnp.where(chosen, 1.0, 0.0).astype(BF16)
        within = jnp.dot(flag, before_lane, preferred_element_type=F32)
        ranks = jnp.dot(before_rank, flag, preferred_element_type=F32).astype(BF16)
        position = within + jnp.dot(ranks, ones, preferred_element_type=F32)
        place = jnp.where(chosen, position + which * LIST, place)
        totals.append(jnp.sum(flag.astype(F32), keepdims=True))
    second = jnp.where(crosses, second - BLOCKS, second)
    target = lax.broadcasted_iota(jnp.int32, (RANKS, LISTS), 1).astype(F32)
    sides = [jnp.zeros((RANKS, LISTS), F32)] * 2
    for slot in range(SLOTS):
        hit = place[:, slot : slot + 1] == target
        sides = [
            kept + jnp.where(hit, side[:, slot : slot + 1] - BLOCKS, 0.0) for kept, side in zip(sides, (first, second))
        ]
    lists = jnp.concatenate([jnp.sum(side, axis=0, keepdims=True) for side in sides], axis=0) + BLOCKS
    for which, total in enumerate(totals):
        lists = jnp.where(target[0:2] == COUNTS + which, total, lists)
    return lists.astype(jnp.int32)


def pieces(x):
    high = x.astype(BF16)
    rest = x - high.astype(F32)
    mid = rest.astype(BF16)
    low = (rest - mid.astype(F32)).astype(BF16)
    return high, mid, low


def radii_of(received, rank):
    return jnp.concatenate([received[rank, 48 + q : 49 + q, :] for q in range(4)], axis=1)


def features(received, rank):
    n = HELD
    radii = radii_of(received, rank)
    row = lax.broadcasted_iota(jnp.int32, (8, n), 0)
    eight = jnp.concatenate([received[rank, 8 * q : 8 * q + 8, :] for q in range(4)], axis=1)
    four = []
    for half in range(2):
        both = received[rank, 32 + 8 * half : 40 + 8 * half, :]
        four += [both, pltpu.roll(both, 4, 0)]
    four = jnp.concatenate(four, axis=1)
    upper = jnp.where(row % 4 == 3, radii, eight)
    lower = jnp.where(row < 3, four, radii)
    for at, moved in ((4, pltpu.roll(eight, 1, 0)), (5, pltpu.roll(eight, 6, 0)), (6, pltpu.roll(four, 3, 0))):
        lower = jnp.where(row == at, moved, lower)
    part = lax.broadcasted_iota(jnp.int32, (16, n), 0) % 4
    values = jnp.concatenate([upper, lower], axis=0)
    square = (values * values).reshape(2, 8, n)
    row = lax.broadcasted_iota(jnp.int32, (2, 8, n), 1)
    twos = square + jnp.where(row % 2 == 1, pltpu.roll(square, 1, 1), pltpu.roll(square, 7, 1))
    fours = twos + jnp.where((row // 2) % 2 == 1, pltpu.roll(twos, 2, 1), pltpu.roll(twos, 6, 1))
    high, mid, low = pieces(values)
    s_high, s_mid, s_low = (p.astype(F32) for p in pieces(fours.reshape(16, n)))
    zero = jnp.zeros((16, n), F32)
    sums = jnp.where(part == 0, s_high, jnp.where(part == 1, s_mid, jnp.where(part == 2, s_low, zero)))
    ones = jnp.where(part == 3, zero, 1.0)
    return high, mid, low, sums, ones, part


def prepare_second(second, second_radii, received, rank):
    high, mid, low, sums, ones, _ = features(received, rank)
    radii = radii_of(received, rank)
    terms = (high, mid, high, low, high, mid, sums.astype(BF16), ones.astype(BF16))
    for i, term in enumerate(terms):
        second[16 * i : 16 * i + 16, rank * HELD : (rank + 1) * HELD] = term
    for half in range(HELD // BLOCK):
        block = rank * (HELD // BLOCK) + half
        second_radii[block : block + 1, :] = radii[:, half * BLOCK : (half + 1) * BLOCK]


def prepare_first(first, first_radii, received, rank):
    high, mid, low, sums, ones, part = features(received, rank)
    radii = radii_of(received, rank)
    scale = jnp.where(part == 3, 2.0, -2.0)
    high, mid, low = (scale * p.astype(F32) for p in (high, mid, low))
    terms = jnp.concatenate([high, high, mid, high, low, mid, ones, sums], axis=0)
    for c in range(0, HELD, 128):
        at = rank * HELD + c
        first[at : at + 128, :] = terms[:, c : c + 128].T.astype(BF16)
        first_radii[at : at + 128, :] = jnp.broadcast_to(radii[:, c : c + 128], (128, 128)).T


def credit_pair(first, first_radii, second, second_radii, rows, columns, a, b):
    from_a = pl.multiple_of(lax.rem(a, BLOCKS) * BLOCK, BLOCK)
    block_b = lax.rem(b, BLOCKS)
    of_b = second[:, pl.ds(pl.multiple_of(block_b * BLOCK, BLOCK), BLOCK)]
    radii_b = second_radii[pl.ds(block_b, 1), :]
    lane = lax.broadcasted_iota(jnp.int32, (TILE, 128), 1)
    masks = [jnp.where((lane % 16) // 4 == t, 1.0, 0.0).astype(BF16) for t in range(4)]
    column = jnp.zeros((8, BLOCK), F32)
    for i in range(0, BLOCK, TILE):
        of_a = first[pl.ds(from_a + i, TILE), :]
        total = None
        for mask in masks:
            whole = jnp.dot(of_a * mask, of_b, preferred_element_type=F32)
            inverse = pl.reciprocal(whole, approx=False)
            total = inverse if total is None else total + inverse
        radii_a = first_radii[pl.ds(from_a + i, TILE), :]
        summed = jnp.concatenate([radii_a, radii_a], axis=1) + radii_b
        weight = total * (summed * summed)
        column = column + jnp.sum(weight.reshape(TILE // 8, 8, BLOCK), axis=0)
        row = jnp.sum(weight[:, :128] + weight[:, 128:], axis=1, keepdims=True)
        rows[i : i + TILE, :] = rows[i : i + TILE, :] + jnp.where(lane == a, row, 0.0)
    at = pl.ds(pl.multiple_of(b * 8, 8), 8)
    columns[at, :] = columns[at, :] + column


def credit_list(first, first_radii, second, second_radii, rows, columns, lists, which):
    @pl.loop(0, (lists[0, COUNTS + which] + UNROLL - 1) // UNROLL)
    def _(step):
        for u in range(UNROLL):
            at = which * LIST + step * UNROLL + u
            credit_pair(first, first_radii, second, second_radii, rows, columns, lists[0, at], lists[1, at])


def block_sums(columns):
    return jnp.sum(columns[0 : 8 * BLOCKS, :].reshape(BLOCKS, 8, BLOCK), axis=1)


def own_kernel(
    received, rows, credited, first, first_radii, lists,
    second, second_radii, columns, listed, sem,
):
    lists[...] = list_pairs(received)
    copy = pltpu.make_async_copy(lists, listed, sem)
    copy.start()
    rows[...] = jnp.zeros_like(rows)
    columns[...] = jnp.zeros_like(columns)
    for rank in range(RANKS):
        prepare_second(second, second_radii, received, rank)
        prepare_first(first, first_radii, received, rank)
    copy.wait()
    credit_list(first, first_radii, second, second_radii, rows, columns, listed, 0)
    credited[...] = block_sums(columns)


def cross_kernel(
    lists, received, earlier_rows, earlier, first, first_radii, out,
    second, second_radii, rows, columns,
):
    rows[...] = earlier_rows[...]
    columns[...] = jnp.zeros_like(columns)
    for rank in range(RANKS):
        prepare_second(second, second_radii, received, rank)
    credit_list(first, first_radii, second, second_radii, rows, columns, lists, 1)
    factor = 1.0 / (TIMES * BLOCK)
    own = (earlier[...] + rows[...].T[0:BLOCKS, :]) * factor
    beyond = block_sums(columns) * factor
    for block in range(BLOCKS):
        rank, half = divmod(block, 2)
        for k in range(2):
            at = 2 * half + k
            out[rank, at : at + 1, :] = own[block : block + 1, k * 128 : (k + 1) * 128]
            out[rank, 4 + at : 5 + at, :] = beyond[block : block + 1, k * 128 : (k + 1) * 128]


def body(coefs, radii, pair_blocks, pair_count):
    in_vmem, in_smem = pl.BlockSpec(memory_space=VMEM), pl.BlockSpec(memory_space=SMEM)
    table = jnp.asarray(spread_table())
    coefs = coefs.transpose(1, 0, 2)
    at_all = pl.pallas_call(
        evaluate_kernel,
        out_shape=jax.ShapeDtypeStruct((RANKS, CHUNK, 128), F32),
        in_specs=[pl.BlockSpec(memory_space=pltpu.HBM)] * 5,
        out_specs=in_vmem,
        scratch_shapes=[
            SMEM(pair_blocks.shape, jnp.int32),
            SMEM(pair_count.shape, jnp.int32),
            VMEM(table.shape, F32),
            VMEM(coefs.shape, F32),
            VMEM(radii.shape, F32),
            pltpu.SemaphoreType.DMA((5,)),
        ],
        compiler_params=pltpu.CompilerParams(vmem_limit_bytes=60 * 1024 * 1024),
        name="evaluate",
    )(pair_blocks, pair_count, table, coefs, radii)
    received = lax.all_to_all(at_all, "rank", 0, 0)
    beyond = passed_along(received, "shell", -1)
    rows, credited, first, first_radii, lists = pl.pallas_call(
        own_kernel,
        out_shape=[
            jax.ShapeDtypeStruct((BLOCK, 128), F32),
            jax.ShapeDtypeStruct((BLOCKS, BLOCK), F32),
            jax.ShapeDtypeStruct((SPAN, 128), BF16),
            jax.ShapeDtypeStruct((SPAN, 128), F32),
            jax.ShapeDtypeStruct((2, LISTS), jnp.int32),
        ],
        in_specs=[in_vmem],
        out_specs=[in_vmem] * 5,
        scratch_shapes=[
            VMEM((128, SPAN), BF16),
            VMEM((BLOCKS, BLOCK), F32),
            VMEM((8 * BLOCKS + 8, BLOCK), F32),
            SMEM((2, LISTS), jnp.int32),
            pltpu.SemaphoreType.DMA,
        ],
        compiler_params=PARAMS,
        cost_estimate=pl.CostEstimate(flops=8_000_000_000, bytes_accessed=8_000_000, transcendentals=0),
        name="own_pairs",
    )(received)
    partial = pl.pallas_call(
        cross_kernel,
        out_shape=jax.ShapeDtypeStruct((RANKS, 8, 128), F32),
        in_specs=[in_smem] + [in_vmem] * 5,
        out_specs=in_vmem,
        scratch_shapes=[
            VMEM((128, SPAN), BF16),
            VMEM((BLOCKS, BLOCK), F32),
            VMEM((BLOCK, 128), F32),
            VMEM((8 * BLOCKS + 8, BLOCK), F32),
        ],
        compiler_params=PARAMS,
        cost_estimate=pl.CostEstimate(flops=8_000_000_000, bytes_accessed=8_000_000, transcendentals=0),
        name="crossing_pairs",
    )(lists, beyond, rows, credited, first, first_radii)
    summed = jnp.sum(lax.all_to_all(partial, "rank", 0, 0), axis=0)
    returned = passed_along(summed[4:], "shell", 1)
    return (summed[:4] + returned).reshape(HELD)


def solution(mesh):
    placed = (
        P(None, None, ("shell", "rank")),
        P(("shell", "rank")),
        P(None, ("shell", "rank")),
        P(("shell", "rank")),
    )
    return jax.shard_map(
        body, mesh=mesh, in_specs=placed, out_specs=P(("shell", "rank")), check_vma=False
    )
```

```python
import jax
import jax.numpy as jnp
import ml_dtypes
import numpy as np
from jax import lax
from jax.experimental import pallas as pl
from jax.experimental.pallas import tpu as pltpu
from jax.sharding import PartitionSpec as P

NCOEF = 16
TIMES = 64
BLOCK = 256
RANKS = 16
SLOTS = 8
BLOCKS = 32
SPAN = BLOCKS * BLOCK
HELD = 512
UNROLL = 16
REST = 4
LIST = 160
LISTS = 512
COUNTS = 480
TILE = 64
F32 = jnp.float32
BF16 = jnp.bfloat16
VMEM = pltpu.VMEM
SMEM = pltpu.SMEM
PARAMS = pltpu.CompilerParams(vmem_limit_bytes=24 * 1024 * 1024)


def passed_along(value, axis, steps):
    count = lax.axis_size(axis)
    leading, last = (max(0, -steps), min(count, count - steps))
    return lax.ppermute(value, axis, [(source, source + steps) for source in range(leading, last)])


EIGHT = ((0, 0), (0, 1), (0, 2), (3, 0), (1, 0), (1, 1), (1, 2), (3, 1))
FOUR = ((2, 0), (2, 1), (2, 2), (3, 2))
CHUNK = 56


def spread_table():
    node = -1.0 + (2.0 * np.arange(TIMES) + 1.0) / TIMES
    table = np.cos(np.arange(NCOEF)[None, :] * np.arccos(node)[:, None])
    spread = np.zeros((RANKS, 16, 3, NCOEF), np.float32)
    for row, (time, coordinate) in enumerate(EIGHT + FOUR + FOUR):
        spread[:, row, coordinate, :] = table[time :: TIMES // RANKS]
    spread = spread.reshape(RANKS * 16, 3 * NCOEF)
    high = spread.astype(ml_dtypes.bfloat16)
    mid = (spread - high.astype(np.float32)).astype(ml_dtypes.bfloat16)
    low = (spread - high.astype(np.float32) - mid.astype(np.float32)).astype(ml_dtypes.bfloat16)
    return np.stack([np.concatenate([high, mid], axis=1), np.concatenate([high, low], axis=1)])


def evaluate_kernel(*refs):
    given, (out, *held, sems) = refs[:5], refs[5:]
    copies = [pltpu.make_async_copy(given[i], held[i], sems.at[i]) for i in range(5)]
    for copy in copies:
        copy.start()
    for copy in copies:
        copy.wait()
    pairs, count, table, coefs, radii = held
    high, mid, low = pieces(coefs[...].reshape(3 * NCOEF, HELD))
    values = None
    for which, above, below in ((0, high, high), (0, mid, mid), (1, low, high)):
        part = jnp.dot(table[which], jnp.concatenate([above, below], axis=0), preferred_element_type=F32)
        values = part if values is None else values + part
    values = values.reshape(RANKS, 16, HELD)
    lane = lax.broadcasted_iota(jnp.int32, (1, 128), 1)
    row = lax.broadcasted_iota(jnp.int32, (8, 128), 0)
    last = jnp.where(row == 6, count[0].astype(F32), 0.0)
    for q in range(4):
        last = jnp.where(row == q, radii[128 * q : 128 * q + 128].reshape(1, 128), last)
    for side in range(2):
        blocks = jnp.zeros((1, 128), F32)
        for slot in range(SLOTS):
            blocks = jnp.where(lane == slot, pairs[side, slot].astype(F32), blocks)
        last = jnp.where(row == 4 + side, blocks, last)
    runs = [values[:, :, 128 * q : 128 * q + 128] for q in range(4)]
    for q in range(4):
        out[:, 8 * q : 8 * q + 8, :] = runs[q][:, 0:8]
    for half in range(2):
        out[:, 32 + 8 * half : 40 + 8 * half, :] = jnp.where(
            row[None] < 4, runs[2 * half][:, 8:16], runs[2 * half + 1][:, 8:16]
        )
    out[:, 48:56, :] = jnp.broadcast_to(last[None], (RANKS, 8, 128))


def list_pairs(received):
    first, second, count = (received[:, row, 0:128] for row in (52, 53, 54))
    lane = lax.broadcasted_iota(jnp.int32, (RANKS, 128), 1)
    live = (lane < SLOTS) & (lane.astype(F32) < count)
    before_lane = jnp.where(
        lax.broadcasted_iota(jnp.int32, (128, 128), 0) < lax.broadcasted_iota(jnp.int32, (128, 128), 1), 1.0, 0.0
    ).astype(BF16)
    before_rank = jnp.where(
        lax.broadcasted_iota(jnp.int32, (RANKS, RANKS), 1) < lax.broadcasted_iota(jnp.int32, (RANKS, RANKS), 0), 1.0, 0.0
    ).astype(BF16)
    ones = jnp.ones((128, 128), BF16)
    crosses = second >= BLOCKS
    place = jnp.full((RANKS, 128), -1.0, F32)
    totals = []
    for which, chosen in enumerate((live & ~crosses, live & crosses)):
        flag = jnp.where(chosen, 1.0, 0.0).astype(BF16)
        within = jnp.dot(flag, before_lane, preferred_element_type=F32)
        ranks = jnp.dot(before_rank, flag, preferred_element_type=F32).astype(BF16)
        position = within + jnp.dot(ranks, ones, preferred_element_type=F32)
        place = jnp.where(chosen, position + which * LIST, place)
        totals.append(jnp.sum(flag.astype(F32), keepdims=True))
    second = jnp.where(crosses, second - BLOCKS, second)
    target = lax.broadcasted_iota(jnp.int32, (RANKS, LISTS), 1).astype(F32)
    sides = [jnp.zeros((RANKS, LISTS), F32)] * 2
    for slot in range(SLOTS):
        hit = place[:, slot : slot + 1] == target
        sides = [
            kept + jnp.where(hit, side[:, slot : slot + 1] - BLOCKS, 0.0) for kept, side in zip(sides, (first, second))
        ]
    lists = jnp.concatenate([jnp.sum(side, axis=0, keepdims=True) for side in sides], axis=0) + BLOCKS
    for which, total in enumerate(totals):
        lists = jnp.where(target[0:2] == COUNTS + which, total, lists)
    return lists.astype(jnp.int32)


def pieces(x):
    high = x.astype(BF16)
    rest = x - high.astype(F32)
    mid = rest.astype(BF16)
    low = (rest - mid.astype(F32)).astype(BF16)
    return high, mid, low


def radii_of(received, rank):
    return jnp.concatenate([received[rank, 48 + q : 49 + q, :] for q in range(4)], axis=1)


def features(received, rank):
    n = HELD
    radii = radii_of(received, rank)
    row = lax.broadcasted_iota(jnp.int32, (8, n), 0)
    eight = jnp.concatenate([received[rank, 8 * q : 8 * q + 8, :] for q in range(4)], axis=1)
    four = []
    for half in range(2):
        both = received[rank, 32 + 8 * half : 40 + 8 * half, :]
        four += [both, pltpu.roll(both, 4, 0)]
    four = jnp.concatenate(four, axis=1)
    upper = jnp.where(row % 4 == 3, radii, eight)
    lower = jnp.where(row < 3, four, radii)
    for at, moved in ((4, pltpu.roll(eight, 1, 0)), (5, pltpu.roll(eight, 6, 0)), (6, pltpu.roll(four, 3, 0))):
        lower = jnp.where(row == at, moved, lower)
    part = lax.broadcasted_iota(jnp.int32, (16, n), 0) % 4
    values = jnp.concatenate([upper, lower], axis=0)
    square = (values * values).reshape(2, 8, n)
    row = lax.broadcasted_iota(jnp.int32, (2, 8, n), 1)
    twos = square + jnp.where(row % 2 == 1, pltpu.roll(square, 1, 1), pltpu.roll(square, 7, 1))
    fours = twos + jnp.where((row // 2) % 2 == 1, pltpu.roll(twos, 2, 1), pltpu.roll(twos, 6, 1))
    high, mid, low = pieces(values)
    s_high, s_mid, s_low = (p.astype(F32) for p in pieces(fours.reshape(16, n)))
    zero = jnp.zeros((16, n), F32)
    sums = jnp.where(part == 0, s_high, jnp.where(part == 1, s_mid, jnp.where(part == 2, s_low, zero)))
    ones = jnp.where(part == 3, zero, 1.0)
    return high, mid, low, sums, ones, part


def prepare_second(second, second_radii, received, rank):
    high, mid, low, sums, ones, _ = features(received, rank)
    radii = radii_of(received, rank)
    terms = (high, mid, high, low, high, mid, sums.astype(BF16), ones.astype(BF16))
    for i, term in enumerate(terms):
        second[16 * i : 16 * i + 16, rank * HELD : (rank + 1) * HELD] = term
    for half in range(HELD // BLOCK):
        block = rank * (HELD // BLOCK) + half
        second_radii[block : block + 1, :] = radii[:, half * BLOCK : (half + 1) * BLOCK]


def prepare_first(first, first_radii, received, rank):
    high, mid, low, sums, ones, part = features(received, rank)
    radii = radii_of(received, rank)
    scale = jnp.where(part == 3, 2.0, -2.0)
    high, mid, low = (scale * p.astype(F32) for p in (high, mid, low))
    terms = jnp.concatenate([high, high, mid, high, low, mid, ones, sums], axis=0)
    for c in range(0, HELD, 128):
        at = rank * HELD + c
        first[at : at + 128, :] = terms[:, c : c + 128].T.astype(BF16)
        first_radii[at : at + 128, :] = jnp.broadcast_to(radii[:, c : c + 128], (128, 128)).T


def credit_pair(first, first_radii, second, second_radii, rows, columns, a, b):
    from_a = pl.multiple_of(lax.rem(a, BLOCKS) * BLOCK, BLOCK)
    block_b = lax.rem(b, BLOCKS)
    of_b = second[:, pl.ds(pl.multiple_of(block_b * BLOCK, BLOCK), BLOCK)]
    radii_b = second_radii[pl.ds(block_b, 1), :]
    lane = lax.broadcasted_iota(jnp.int32, (TILE, 128), 1)
    masks = [jnp.where((lane % 16) // 4 == t, 1.0, 0.0).astype(BF16) for t in range(4)]
    column = jnp.zeros((8, BLOCK), F32)
    for i in range(0, BLOCK, TILE):
        of_a = first[pl.ds(from_a + i, TILE), :]
        total = None
        for mask in masks:
            whole = jnp.dot(of_a * mask, of_b, preferred_element_type=F32)
            inverse = pl.reciprocal(whole, approx=False)
            total = inverse if total is None else total + inverse
        radii_a = first_radii[pl.ds(from_a + i, TILE), :]
        summed = jnp.concatenate([radii_a, radii_a], axis=1) + radii_b
        weight = total * (summed * summed)
        column = column + jnp.sum(weight.reshape(TILE // 8, 8, BLOCK), axis=0)
        row = jnp.sum(weight[:, :128] + weight[:, 128:], axis=1, keepdims=True)
        rows[i : i + TILE, :] = rows[i : i + TILE, :] + jnp.where(lane == a, row, 0.0)
    at = pl.ds(pl.multiple_of(b * 8, 8), 8)
    columns[at, :] = columns[at, :] + column


def credit_list(first, first_radii, second, second_radii, rows, columns, lists, which):
    count = lists[0, COUNTS + which]
    whole = count // UNROLL

    def steps(start, stop, pairs):
        @pl.loop(start, stop)
        def _(step):
            for u in range(pairs):
                at = which * LIST + step * pairs + u
                credit_pair(first, first_radii, second, second_radii, rows, columns, lists[0, at], lists[1, at])

    steps(0, whole, UNROLL)
    steps(whole * (UNROLL // REST), (count + REST - 1) // REST, REST)


def block_sums(columns):
    return jnp.sum(columns[0 : 8 * BLOCKS, :].reshape(BLOCKS, 8, BLOCK), axis=1)


def own_kernel(
    received, rows, credited, first, first_radii, lists,
    second, second_radii, columns, listed, sem,
):
    lists[...] = list_pairs(received)
    copy = pltpu.make_async_copy(lists, listed, sem)
    copy.start()
    rows[...] = jnp.zeros_like(rows)
    columns[...] = jnp.zeros_like(columns)
    for rank in range(RANKS):
        prepare_second(second, second_radii, received, rank)
        prepare_first(first, first_radii, received, rank)
    copy.wait()
    credit_list(first, first_radii, second, second_radii, rows, columns, listed, 0)
    credited[...] = block_sums(columns)


def cross_kernel(
    lists, received, earlier_rows, earlier, first, first_radii, out,
    second, second_radii, rows, columns,
):
    rows[...] = earlier_rows[...]
    columns[...] = jnp.zeros_like(columns)
    for rank in range(RANKS):
        prepare_second(second, second_radii, received, rank)
    credit_list(first, first_radii, second, second_radii, rows, columns, lists, 1)
    factor = 1.0 / (TIMES * BLOCK)
    own = (earlier[...] + rows[...].T[0:BLOCKS, :]) * factor
    beyond = block_sums(columns) * factor
    for block in range(BLOCKS):
        rank, half = divmod(block, 2)
        for k in range(2):
            at = 2 * half + k
            out[rank, at : at + 1, :] = own[block : block + 1, k * 128 : (k + 1) * 128]
            out[rank, 4 + at : 5 + at, :] = beyond[block : block + 1, k * 128 : (k + 1) * 128]


def body(coefs, radii, pair_blocks, pair_count):
    in_vmem, in_smem = pl.BlockSpec(memory_space=VMEM), pl.BlockSpec(memory_space=SMEM)
    table = jnp.asarray(spread_table())
    coefs = coefs.transpose(1, 0, 2)
    at_all = pl.pallas_call(
        evaluate_kernel,
        out_shape=jax.ShapeDtypeStruct((RANKS, CHUNK, 128), F32),
        in_specs=[pl.BlockSpec(memory_space=pltpu.HBM)] * 5,
        out_specs=in_vmem,
        scratch_shapes=[
            SMEM(pair_blocks.shape, jnp.int32),
            SMEM(pair_count.shape, jnp.int32),
            VMEM(table.shape, BF16),
            VMEM(coefs.shape, F32),
            VMEM(radii.shape, F32),
            pltpu.SemaphoreType.DMA((5,)),
        ],
        compiler_params=pltpu.CompilerParams(vmem_limit_bytes=60 * 1024 * 1024),
        name="evaluate",
    )(pair_blocks, pair_count, table, coefs, radii)
    received = lax.all_to_all(at_all, "rank", 0, 0)
    beyond = passed_along(received, "shell", -1)
    rows, credited, first, first_radii, lists = pl.pallas_call(
        own_kernel,
        out_shape=[
            jax.ShapeDtypeStruct((BLOCK, 128), F32),
            jax.ShapeDtypeStruct((BLOCKS, BLOCK), F32),
            jax.ShapeDtypeStruct((SPAN, 128), BF16),
            jax.ShapeDtypeStruct((SPAN, 128), F32),
            jax.ShapeDtypeStruct((2, LISTS), jnp.int32),
        ],
        in_specs=[in_vmem],
        out_specs=[in_vmem] * 5,
        scratch_shapes=[
            VMEM((128, SPAN), BF16),
            VMEM((BLOCKS, BLOCK), F32),
            VMEM((8 * BLOCKS + 8, BLOCK), F32),
            SMEM((2, LISTS), jnp.int32),
            pltpu.SemaphoreType.DMA,
        ],
        compiler_params=PARAMS,
        cost_estimate=pl.CostEstimate(flops=8_000_000_000, bytes_accessed=8_000_000, transcendentals=0),
        name="own_pairs",
    )(received)
    partial = pl.pallas_call(
        cross_kernel,
        out_shape=jax.ShapeDtypeStruct((RANKS, 8, 128), F32),
        in_specs=[in_smem] + [in_vmem] * 5,
        out_specs=in_vmem,
        scratch_shapes=[
            VMEM((128, SPAN), BF16),
            VMEM((BLOCKS, BLOCK), F32),
            VMEM((BLOCK, 128), F32),
            VMEM((8 * BLOCKS + 8, BLOCK), F32),
        ],
        compiler_params=PARAMS,
        cost_estimate=pl.CostEstimate(flops=8_000_000_000, bytes_accessed=8_000_000, transcendentals=0),
        name="crossing_pairs",
    )(lists, beyond, rows, credited, first, first_radii)
    summed = jnp.sum(lax.all_to_all(partial, "rank", 0, 0), axis=0)
    returned = passed_along(summed[4:], "shell", 1)
    return (summed[:4] + returned).reshape(HELD)


def solution(mesh):
    placed = (
        P(None, None, ("shell", "rank")),
        P(("shell", "rank")),
        P(None, ("shell", "rank")),
        P(("shell", "rank")),
    )
    return jax.shard_map(
        body, mesh=mesh, in_specs=placed, out_specs=P(("shell", "rank")), check_vma=False
    )
```

```python
import jax
import jax.numpy as jnp
import ml_dtypes
import numpy as np
from jax import lax
from jax.experimental import pallas as pl
from jax.experimental.pallas import tpu as pltpu
from jax.sharding import PartitionSpec as P

NCOEF = 16
TIMES = 64
BLOCK = 256
RANKS = 16
SLOTS = 8
BLOCKS = 32
SPAN = BLOCKS * BLOCK
HELD = 512
UNROLL = 16
REST = 4
LIST = 160
LISTS = 512
COUNTS = 480
TILE = 64
F32 = jnp.float32
BF16 = jnp.bfloat16
VMEM = pltpu.VMEM
SMEM = pltpu.SMEM
PARAMS = pltpu.CompilerParams(vmem_limit_bytes=24 * 1024 * 1024)


def passed_along(value, axis, steps):
    count = lax.axis_size(axis)
    leading, last = (max(0, -steps), min(count, count - steps))
    return lax.ppermute(value, axis, [(source, source + steps) for source in range(leading, last)])


EIGHT = ((0, 0), (0, 1), (0, 2), (3, 0), (1, 0), (1, 1), (1, 2), (3, 1))
FOUR = ((2, 0), (2, 1), (2, 2), (3, 2))
CHUNK = 56


def spread_table():
    node = -1.0 + (2.0 * np.arange(TIMES) + 1.0) / TIMES
    table = np.cos(np.arange(NCOEF)[None, :] * np.arccos(node)[:, None])
    spread = np.zeros((RANKS, 16, 3, NCOEF), np.float32)
    for row, (time, coordinate) in enumerate(EIGHT + FOUR + FOUR):
        spread[:, row, coordinate, :] = table[time :: TIMES // RANKS]
    spread = spread.reshape(RANKS * 16, 3 * NCOEF)
    high = spread.astype(ml_dtypes.bfloat16)
    mid = (spread - high.astype(np.float32)).astype(ml_dtypes.bfloat16)
    low = (spread - high.astype(np.float32) - mid.astype(np.float32)).astype(ml_dtypes.bfloat16)
    return np.stack([np.concatenate([high, mid], axis=1), np.concatenate([high, low], axis=1)])


def evaluate_kernel(*refs):
    given, (out, *held, sems) = refs[:5], refs[5:]
    copies = [pltpu.make_async_copy(given[i], held[i], sems.at[i]) for i in range(5)]
    for copy in copies:
        copy.start()
    for copy in copies:
        copy.wait()
    pairs, count, table, coefs, radii = held
    high, mid, low = pieces(coefs[...].reshape(3 * NCOEF, HELD))
    values = None
    for which, above, below in ((0, high, high), (0, mid, mid), (1, low, high)):
        part = jnp.dot(table[which], jnp.concatenate([above, below], axis=0), preferred_element_type=F32)
        values = part if values is None else values + part
    values = values.reshape(RANKS, 16, HELD)
    lane = lax.broadcasted_iota(jnp.int32, (1, 128), 1)
    row = lax.broadcasted_iota(jnp.int32, (8, 128), 0)
    last = jnp.where(row == 6, count[0].astype(F32), 0.0)
    for q in range(4):
        last = jnp.where(row == q, radii[128 * q : 128 * q + 128].reshape(1, 128), last)
    for side in range(2):
        blocks = jnp.zeros((1, 128), F32)
        for slot in range(SLOTS):
            blocks = jnp.where(lane == slot, pairs[side, slot].astype(F32), blocks)
        last = jnp.where(row == 4 + side, blocks, last)
    runs = [values[:, :, 128 * q : 128 * q + 128] for q in range(4)]
    for q in range(4):
        out[:, 8 * q : 8 * q + 8, :] = runs[q][:, 0:8]
    for half in range(2):
        out[:, 32 + 8 * half : 40 + 8 * half, :] = jnp.where(
            row[None] < 4, runs[2 * half][:, 8:16], runs[2 * half + 1][:, 8:16]
        )
    out[:, 48:56, :] = jnp.broadcast_to(last[None], (RANKS, 8, 128))


def list_pairs(received):
    first, second, count = (received[:, row, 0:128] for row in (52, 53, 54))
    lane = lax.broadcasted_iota(jnp.int32, (RANKS, 128), 1)
    live = (lane < SLOTS) & (lane.astype(F32) < count)
    before_lane = jnp.where(
        lax.broadcasted_iota(jnp.int32, (128, 128), 0) < lax.broadcasted_iota(jnp.int32, (128, 128), 1), 1.0, 0.0
    ).astype(BF16)
    before_rank = jnp.where(
        lax.broadcasted_iota(jnp.int32, (RANKS, RANKS), 1) < lax.broadcasted_iota(jnp.int32, (RANKS, RANKS), 0), 1.0, 0.0
    ).astype(BF16)
    ones = jnp.ones((128, 128), BF16)
    crosses = second >= BLOCKS
    place = jnp.full((RANKS, 128), -1.0, F32)
    totals = []
    for which, chosen in enumerate((live & ~crosses, live & crosses)):
        flag = jnp.where(chosen, 1.0, 0.0).astype(BF16)
        within = jnp.dot(flag, before_lane, preferred_element_type=F32)
        ranks = jnp.dot(before_rank, flag, preferred_element_type=F32).astype(BF16)
        position = within + jnp.dot(ranks, ones, preferred_element_type=F32)
        place = jnp.where(chosen, position + which * LIST, place)
        totals.append(jnp.sum(flag.astype(F32), keepdims=True))
    second = jnp.where(crosses, second - BLOCKS, second)
    target = lax.broadcasted_iota(jnp.int32, (RANKS, LISTS), 1).astype(F32)
    sides = [jnp.zeros((RANKS, LISTS), F32)] * 2
    for slot in range(SLOTS):
        hit = place[:, slot : slot + 1] == target
        sides = [
            kept + jnp.where(hit, side[:, slot : slot + 1] - BLOCKS, 0.0) for kept, side in zip(sides, (first, second))
        ]
    lists = jnp.concatenate([jnp.sum(side, axis=0, keepdims=True) for side in sides], axis=0) + BLOCKS
    for which, total in enumerate(totals):
        lists = jnp.where(target[0:2] == COUNTS + which, total, lists)
    return lists.astype(jnp.int32)


def pieces(x):
    high = x.astype(BF16)
    rest = x - high.astype(F32)
    mid = rest.astype(BF16)
    low = (rest - mid.astype(F32)).astype(BF16)
    return high, mid, low


def radii_of(received, rank):
    return jnp.concatenate([received[rank, 48 + q : 49 + q, :] for q in range(4)], axis=1)


def features(received, rank):
    n = HELD
    radii = radii_of(received, rank)
    row = lax.broadcasted_iota(jnp.int32, (8, n), 0)
    eight = jnp.concatenate([received[rank, 8 * q : 8 * q + 8, :] for q in range(4)], axis=1)
    four = []
    for half in range(2):
        both = received[rank, 32 + 8 * half : 40 + 8 * half, :]
        four += [both, pltpu.roll(both, 4, 0)]
    four = jnp.concatenate(four, axis=1)
    upper = jnp.where(row % 4 == 3, radii, eight)
    lower = jnp.where(row < 3, four, radii)
    for at, moved in ((4, pltpu.roll(eight, 1, 0)), (5, pltpu.roll(eight, 6, 0)), (6, pltpu.roll(four, 3, 0))):
        lower = jnp.where(row == at, moved, lower)
    part = lax.broadcasted_iota(jnp.int32, (16, n), 0) % 4
    values = jnp.concatenate([upper, lower], axis=0)
    square = (values * values).reshape(2, 8, n)
    row = lax.broadcasted_iota(jnp.int32, (2, 8, n), 1)
    twos = square + jnp.where(row % 2 == 1, pltpu.roll(square, 1, 1), pltpu.roll(square, 7, 1))
    fours = twos + jnp.where((row // 2) % 2 == 1, pltpu.roll(twos, 2, 1), pltpu.roll(twos, 6, 1))
    high, mid, low = pieces(values)
    s_high, s_mid, s_low = (p.astype(F32) for p in pieces(fours.reshape(16, n)))
    zero = jnp.zeros((16, n), F32)
    sums = jnp.where(part == 0, s_high, jnp.where(part == 1, s_mid, jnp.where(part == 2, s_low, zero)))
    ones = jnp.where(part == 3, zero, 1.0)
    return high, mid, low, sums, ones, part


def prepare_second(second, second_radii, received, rank):
    high, mid, low, sums, ones, _ = features(received, rank)
    radii = radii_of(received, rank)
    terms = (high, mid, high, low, high, mid, sums.astype(BF16), ones.astype(BF16))
    for i, term in enumerate(terms):
        second[16 * i : 16 * i + 16, rank * HELD : (rank + 1) * HELD] = term
    for half in range(HELD // BLOCK):
        block = rank * (HELD // BLOCK) + half
        second_radii[block : block + 1, :] = radii[:, half * BLOCK : (half + 1) * BLOCK]


def prepare_first(first, first_radii, received, rank):
    high, mid, low, sums, ones, part = features(received, rank)
    radii = radii_of(received, rank)
    scale = jnp.where(part == 3, 2.0, -2.0)
    high, mid, low = (scale * p.astype(F32) for p in (high, mid, low))
    terms = jnp.concatenate([high, high, mid, high, low, mid, ones, sums], axis=0)
    for c in range(0, HELD, 128):
        at = rank * HELD + c
        first[at : at + 128, :] = terms[:, c : c + 128].T.astype(BF16)
        first_radii[at : at + 128, :] = jnp.broadcast_to(radii[:, c : c + 128], (128, 128)).T


def credit_pair(first, first_radii, second, second_radii, rows, columns, a, b):
    from_a = pl.multiple_of(lax.rem(a, BLOCKS) * BLOCK, BLOCK)
    block_b = lax.rem(b, BLOCKS)
    of_b = second[:, pl.ds(pl.multiple_of(block_b * BLOCK, BLOCK), BLOCK)]
    radii_b = second_radii[pl.ds(block_b, 1), :]
    lane = lax.broadcasted_iota(jnp.int32, (TILE, 128), 1)
    masks = [jnp.where((lane % 16) // 4 == t, 1.0, 0.0).astype(BF16) for t in range(4)]
    column = jnp.zeros((8, BLOCK), F32)
    for i in range(0, BLOCK, TILE):
        of_a = first[pl.ds(from_a + i, TILE), :]
        total = None
        for mask in masks:
            whole = jnp.dot(of_a * mask, of_b, preferred_element_type=F32)
            inverse = pl.reciprocal(whole, approx=False)
            total = inverse if total is None else total + inverse
        radii_a = first_radii[pl.ds(from_a + i, TILE), :]
        summed = jnp.concatenate([radii_a, radii_a], axis=1) + radii_b
        weight = total * (summed * summed)
        column = column + jnp.sum(weight.reshape(TILE // 8, 8, BLOCK), axis=0)
        row = jnp.sum(weight[:, :128] + weight[:, 128:], axis=1, keepdims=True)
        rows[i : i + TILE, :] = rows[i : i + TILE, :] + jnp.where(lane == a, row, 0.0)
    at = pl.ds(pl.multiple_of(b * 8, 8), 8)
    columns[at, :] = columns[at, :] + column


def credit_list(first, first_radii, second, second_radii, rows, columns, lists, which):
    count = lists[0, COUNTS + which]
    whole = count // UNROLL

    def steps(start, stop, pairs):
        @pl.loop(start, stop)
        def _(step):
            for u in range(pairs):
                at = which * LIST + step * pairs + u
                credit_pair(first, first_radii, second, second_radii, rows, columns, lists[0, at], lists[1, at])

    steps(0, whole, UNROLL)
    steps(whole * (UNROLL // REST), (count + REST - 1) // REST, REST)


def block_sums(columns):
    return jnp.sum(columns[0 : 8 * BLOCKS, :].reshape(BLOCKS, 8, BLOCK), axis=1)


def own_kernel(
    received, rows, credited, first, first_radii, lists,
    second, second_radii, columns, listed, sem,
):
    lists[...] = list_pairs(received)
    copy = pltpu.make_async_copy(lists, listed, sem)
    copy.start()
    rows[...] = jnp.zeros_like(rows)
    columns[...] = jnp.zeros_like(columns)
    for rank in range(RANKS):
        prepare_second(second, second_radii, received, rank)
        prepare_first(first, first_radii, received, rank)
    copy.wait()
    credit_list(first, first_radii, second, second_radii, rows, columns, listed, 0)
    credited[...] = block_sums(columns)


def cross_kernel(
    lists, received, earlier_rows, earlier, first, first_radii, out,
    second, second_radii, rows, columns, listed, sem,
):
    copy = pltpu.make_async_copy(lists, listed, sem)
    copy.start()
    rows[...] = earlier_rows[...]
    columns[...] = jnp.zeros_like(columns)
    for rank in range(RANKS):
        prepare_second(second, second_radii, received, rank)
    copy.wait()
    credit_list(first, first_radii, second, second_radii, rows, columns, listed, 1)
    factor = 1.0 / (TIMES * BLOCK)
    own = (earlier[...] + rows[...].T[0:BLOCKS, :]) * factor
    beyond = block_sums(columns) * factor
    for block in range(BLOCKS):
        rank, half = divmod(block, 2)
        for k in range(2):
            at = 2 * half + k
            out[rank, at : at + 1, :] = own[block : block + 1, k * 128 : (k + 1) * 128]
            out[rank, 4 + at : 5 + at, :] = beyond[block : block + 1, k * 128 : (k + 1) * 128]


def body(coefs, radii, pair_blocks, pair_count):
    in_vmem = pl.BlockSpec(memory_space=VMEM)
    table = jnp.asarray(spread_table())
    coefs = coefs.transpose(1, 0, 2)
    at_all = pl.pallas_call(
        evaluate_kernel,
        out_shape=jax.ShapeDtypeStruct((RANKS, CHUNK, 128), F32),
        in_specs=[pl.BlockSpec(memory_space=pltpu.HBM)] * 5,
        out_specs=in_vmem,
        scratch_shapes=[
            SMEM(pair_blocks.shape, jnp.int32),
            SMEM(pair_count.shape, jnp.int32),
            VMEM(table.shape, BF16),
            VMEM(coefs.shape, F32),
            VMEM(radii.shape, F32),
            pltpu.SemaphoreType.DMA((5,)),
        ],
        compiler_params=pltpu.CompilerParams(vmem_limit_bytes=60 * 1024 * 1024),
        name="evaluate",
    )(pair_blocks, pair_count, table, coefs, radii)
    received = lax.all_to_all(at_all, "rank", 0, 0)
    beyond = passed_along(received, "shell", -1)
    rows, credited, first, first_radii, lists = pl.pallas_call(
        own_kernel,
        out_shape=[
            jax.ShapeDtypeStruct((BLOCK, 128), F32),
            jax.ShapeDtypeStruct((BLOCKS, BLOCK), F32),
            jax.ShapeDtypeStruct((SPAN, 128), BF16),
            jax.ShapeDtypeStruct((SPAN, 128), F32),
            jax.ShapeDtypeStruct((2, LISTS), jnp.int32),
        ],
        in_specs=[in_vmem],
        out_specs=[in_vmem] * 5,
        scratch_shapes=[
            VMEM((128, SPAN), BF16),
            VMEM((BLOCKS, BLOCK), F32),
            VMEM((8 * BLOCKS + 8, BLOCK), F32),
            SMEM((2, LISTS), jnp.int32),
            pltpu.SemaphoreType.DMA,
        ],
        compiler_params=PARAMS,
        cost_estimate=pl.CostEstimate(flops=8_000_000_000, bytes_accessed=8_000_000, transcendentals=0),
        name="own_pairs",
    )(received)
    partial = pl.pallas_call(
        cross_kernel,
        out_shape=jax.ShapeDtypeStruct((RANKS, 8, 128), F32),
        in_specs=[in_vmem] * 6,
        out_specs=in_vmem,
        scratch_shapes=[
            VMEM((128, SPAN), BF16),
            VMEM((BLOCKS, BLOCK), F32),
            VMEM((BLOCK, 128), F32),
            VMEM((8 * BLOCKS + 8, BLOCK), F32),
            SMEM((2, LISTS), jnp.int32),
            pltpu.SemaphoreType.DMA,
        ],
        compiler_params=PARAMS,
        cost_estimate=pl.CostEstimate(flops=8_000_000_000, bytes_accessed=8_000_000, transcendentals=0),
        name="crossing_pairs",
    )(lists, beyond, rows, credited, first, first_radii)
    summed = jnp.sum(lax.all_to_all(partial, "rank", 0, 0), axis=0)
    returned = passed_along(summed[4:], "shell", 1)
    return (summed[:4] + returned).reshape(HELD)


def solution(mesh):
    placed = (
        P(None, None, ("shell", "rank")),
        P(("shell", "rank")),
        P(None, ("shell", "rank")),
        P(("shell", "rank")),
    )
    return jax.shard_map(
        body, mesh=mesh, in_specs=placed, out_specs=P(("shell", "rank")), check_vma=False
    )
```

```python
import jax
import jax.numpy as jnp
import ml_dtypes
import numpy as np
from jax import lax
from jax.experimental import pallas as pl
from jax.experimental.pallas import tpu as pltpu
from jax.sharding import PartitionSpec as P

NCOEF = 16
TIMES = 64
BLOCK = 256
RANKS = 16
SLOTS = 8
BLOCKS = 32
SPAN = BLOCKS * BLOCK
HELD = 512
UNROLL = 16
REST = 4
LIST = 160
LISTS = 512
COUNTS = 480
TILE = 64
F32 = jnp.float32
BF16 = jnp.bfloat16
VMEM = pltpu.VMEM
SMEM = pltpu.SMEM
PARAMS = pltpu.CompilerParams(vmem_limit_bytes=24 * 1024 * 1024)


def passed_along(value, axis, steps):
    count = lax.axis_size(axis)
    leading, last = (max(0, -steps), min(count, count - steps))
    return lax.ppermute(value, axis, [(source, source + steps) for source in range(leading, last)])


EIGHT = ((0, 0), (0, 1), (0, 2), (3, 0), (1, 0), (1, 1), (1, 2), (3, 1))
FOUR = ((2, 0), (2, 1), (2, 2), (3, 2))
CHUNK = 56


def spread_table():
    node = -1.0 + (2.0 * np.arange(TIMES) + 1.0) / TIMES
    table = np.cos(np.arange(NCOEF)[None, :] * np.arccos(node)[:, None])
    spread = np.zeros((RANKS, 16, 3, NCOEF), np.float32)
    for row, (time, coordinate) in enumerate(EIGHT + FOUR + FOUR):
        spread[:, row, coordinate, :] = table[time :: TIMES // RANKS]
    spread = spread.reshape(RANKS * 16, 3 * NCOEF)
    high = spread.astype(ml_dtypes.bfloat16)
    mid = (spread - high.astype(np.float32)).astype(ml_dtypes.bfloat16)
    low = (spread - high.astype(np.float32) - mid.astype(np.float32)).astype(ml_dtypes.bfloat16)
    return np.stack([np.concatenate([high, mid], axis=1), np.concatenate([high, low], axis=1)])


def evaluate_kernel(*refs):
    count, *given = refs[:5]
    out, *held, sems = refs[5:]
    copies = [pltpu.make_async_copy(given[i], held[i], sems.at[i]) for i in range(4)]
    for copy in copies:
        copy.start()
    for copy in copies:
        copy.wait()
    pairs, table, coefs, radii = held
    high, mid, low = pieces(coefs[...].reshape(3 * NCOEF, HELD))
    values = None
    for which, above, below in ((0, high, high), (0, mid, mid), (1, low, high)):
        part = jnp.dot(table[which], jnp.concatenate([above, below], axis=0), preferred_element_type=F32)
        values = part if values is None else values + part
    values = values.reshape(RANKS, 16, HELD)
    lane = lax.broadcasted_iota(jnp.int32, (1, 128), 1)
    row = lax.broadcasted_iota(jnp.int32, (8, 128), 0)
    last = jnp.where(row == 6, count[0].astype(F32), 0.0)
    for q in range(4):
        last = jnp.where(row == q, radii[128 * q : 128 * q + 128].reshape(1, 128), last)
    for side in range(2):
        blocks = jnp.zeros((1, 128), F32)
        for slot in range(SLOTS):
            blocks = jnp.where(lane == slot, pairs[side, slot].astype(F32), blocks)
        last = jnp.where(row == 4 + side, blocks, last)
    runs = [values[:, :, 128 * q : 128 * q + 128] for q in range(4)]
    for q in range(4):
        out[:, 8 * q : 8 * q + 8, :] = runs[q][:, 0:8]
    for half in range(2):
        out[:, 32 + 8 * half : 40 + 8 * half, :] = jnp.where(
            row[None] < 4, runs[2 * half][:, 8:16], runs[2 * half + 1][:, 8:16]
        )
    out[:, 48:56, :] = jnp.broadcast_to(last[None], (RANKS, 8, 128))


def list_pairs(received):
    first, second, count = (received[:, row, 0:128] for row in (52, 53, 54))
    lane = lax.broadcasted_iota(jnp.int32, (RANKS, 128), 1)
    live = (lane < SLOTS) & (lane.astype(F32) < count)
    before_lane = jnp.where(
        lax.broadcasted_iota(jnp.int32, (128, 128), 0) < lax.broadcasted_iota(jnp.int32, (128, 128), 1), 1.0, 0.0
    ).astype(BF16)
    before_rank = jnp.where(
        lax.broadcasted_iota(jnp.int32, (RANKS, RANKS), 1) < lax.broadcasted_iota(jnp.int32, (RANKS, RANKS), 0), 1.0, 0.0
    ).astype(BF16)
    ones = jnp.ones((128, 128), BF16)
    crosses = second >= BLOCKS
    place = jnp.full((RANKS, 128), -1.0, F32)
    totals = []
    for which, chosen in enumerate((live & ~crosses, live & crosses)):
        flag = jnp.where(chosen, 1.0, 0.0).astype(BF16)
        within = jnp.dot(flag, before_lane, preferred_element_type=F32)
        ranks = jnp.dot(before_rank, flag, preferred_element_type=F32).astype(BF16)
        position = within + jnp.dot(ranks, ones, preferred_element_type=F32)
        place = jnp.where(chosen, position + which * LIST, place)
        totals.append(jnp.sum(flag.astype(F32), keepdims=True))
    second = jnp.where(crosses, second - BLOCKS, second)
    target = lax.broadcasted_iota(jnp.int32, (RANKS, LISTS), 1).astype(F32)
    sides = [jnp.zeros((RANKS, LISTS), F32)] * 2
    for slot in range(SLOTS):
        hit = place[:, slot : slot + 1] == target
        sides = [
            kept + jnp.where(hit, side[:, slot : slot + 1] - BLOCKS, 0.0) for kept, side in zip(sides, (first, second))
        ]
    lists = jnp.concatenate([jnp.sum(side, axis=0, keepdims=True) for side in sides], axis=0) + BLOCKS
    for which, total in enumerate(totals):
        lists = jnp.where(target[0:2] == COUNTS + which, total, lists)
    return lists.astype(jnp.int32)


def pieces(x):
    high = x.astype(BF16)
    rest = x - high.astype(F32)
    mid = rest.astype(BF16)
    low = (rest - mid.astype(F32)).astype(BF16)
    return high, mid, low


def radii_of(received, rank):
    return jnp.concatenate([received[rank, 48 + q : 49 + q, :] for q in range(4)], axis=1)


def features(received, rank):
    n = HELD
    radii = radii_of(received, rank)
    row = lax.broadcasted_iota(jnp.int32, (8, n), 0)
    eight = jnp.concatenate([received[rank, 8 * q : 8 * q + 8, :] for q in range(4)], axis=1)
    four = []
    for half in range(2):
        both = received[rank, 32 + 8 * half : 40 + 8 * half, :]
        four += [both, pltpu.roll(both, 4, 0)]
    four = jnp.concatenate(four, axis=1)
    upper = jnp.where(row % 4 == 3, radii, eight)
    lower = jnp.where(row < 3, four, radii)
    for at, moved in ((4, pltpu.roll(eight, 1, 0)), (5, pltpu.roll(eight, 6, 0)), (6, pltpu.roll(four, 3, 0))):
        lower = jnp.where(row == at, moved, lower)
    part = lax.broadcasted_iota(jnp.int32, (16, n), 0) % 4
    values = jnp.concatenate([upper, lower], axis=0)
    square = (values * values).reshape(2, 8, n)
    row = lax.broadcasted_iota(jnp.int32, (2, 8, n), 1)
    twos = square + jnp.where(row % 2 == 1, pltpu.roll(square, 1, 1), pltpu.roll(square, 7, 1))
    fours = twos + jnp.where((row // 2) % 2 == 1, pltpu.roll(twos, 2, 1), pltpu.roll(twos, 6, 1))
    high, mid, low = pieces(values)
    s_high, s_mid, s_low = (p.astype(F32) for p in pieces(fours.reshape(16, n)))
    zero = jnp.zeros((16, n), F32)
    sums = jnp.where(part == 0, s_high, jnp.where(part == 1, s_mid, jnp.where(part == 2, s_low, zero)))
    ones = jnp.where(part == 3, zero, 1.0)
    return high, mid, low, sums, ones, part


def prepare_second(second, second_radii, received, rank):
    high, mid, low, sums, ones, _ = features(received, rank)
    radii = radii_of(received, rank)
    terms = (high, mid, high, low, high, mid, sums.astype(BF16), ones.astype(BF16))
    for i, term in enumerate(terms):
        second[16 * i : 16 * i + 16, rank * HELD : (rank + 1) * HELD] = term
    for half in range(HELD // BLOCK):
        block = rank * (HELD // BLOCK) + half
        second_radii[block : block + 1, :] = radii[:, half * BLOCK : (half + 1) * BLOCK]


def prepare_first(first, first_radii, received, rank):
    high, mid, low, sums, ones, part = features(received, rank)
    radii = radii_of(received, rank)
    scale = jnp.where(part == 3, 2.0, -2.0)
    high, mid, low = (scale * p.astype(F32) for p in (high, mid, low))
    terms = jnp.concatenate([high, high, mid, high, low, mid, ones, sums], axis=0)
    for c in range(0, HELD, 128):
        at = rank * HELD + c
        first[at : at + 128, :] = terms[:, c : c + 128].T.astype(BF16)
        first_radii[at : at + 128, :] = jnp.broadcast_to(radii[:, c : c + 128], (128, 128)).T


def credit_pair(first, first_radii, second, second_radii, rows, columns, a, b):
    from_a = pl.multiple_of(lax.rem(a, BLOCKS) * BLOCK, BLOCK)
    block_b = lax.rem(b, BLOCKS)
    of_b = second[:, pl.ds(pl.multiple_of(block_b * BLOCK, BLOCK), BLOCK)]
    radii_b = second_radii[pl.ds(block_b, 1), :]
    lane = lax.broadcasted_iota(jnp.int32, (TILE, 128), 1)
    masks = [jnp.where((lane % 16) // 4 == t, 1.0, 0.0).astype(BF16) for t in range(4)]
    column = jnp.zeros((8, BLOCK), F32)
    for i in range(0, BLOCK, TILE):
        of_a = first[pl.ds(from_a + i, TILE), :]
        total = None
        for mask in masks:
            whole = jnp.dot(of_a * mask, of_b, preferred_element_type=F32)
            inverse = pl.reciprocal(whole, approx=False)
            total = inverse if total is None else total + inverse
        radii_a = first_radii[pl.ds(from_a + i, TILE), :]
        summed = jnp.concatenate([radii_a, radii_a], axis=1) + radii_b
        weight = total * (summed * summed)
        column = column + jnp.sum(weight.reshape(TILE // 8, 8, BLOCK), axis=0)
        row = jnp.sum(weight[:, :128] + weight[:, 128:], axis=1, keepdims=True)
        rows[i : i + TILE, :] = rows[i : i + TILE, :] + jnp.where(lane == a, row, 0.0)
    at = pl.ds(pl.multiple_of(b * 8, 8), 8)
    columns[at, :] = columns[at, :] + column


def credit_list(first, first_radii, second, second_radii, rows, columns, lists, which):
    count = lists[0, COUNTS + which]
    whole = count // UNROLL

    def steps(start, stop, pairs):
        @pl.loop(start, stop)
        def _(step):
            for u in range(pairs):
                at = which * LIST + step * pairs + u
                credit_pair(first, first_radii, second, second_radii, rows, columns, lists[0, at], lists[1, at])

    steps(0, whole, UNROLL)
    steps(whole * (UNROLL // REST), (count + REST - 1) // REST, REST)


def block_sums(columns):
    return jnp.sum(columns[0 : 8 * BLOCKS, :].reshape(BLOCKS, 8, BLOCK), axis=1)


def own_kernel(
    received, rows, credited, first, first_radii, lists,
    second, second_radii, columns, listed, sem,
):
    lists[...] = list_pairs(received)
    copy = pltpu.make_async_copy(lists, listed, sem)
    copy.start()
    rows[...] = jnp.zeros_like(rows)
    columns[...] = jnp.zeros_like(columns)
    for rank in range(RANKS):
        prepare_second(second, second_radii, received, rank)
        prepare_first(first, first_radii, received, rank)
    copy.wait()
    credit_list(first, first_radii, second, second_radii, rows, columns, listed, 0)
    credited[...] = block_sums(columns)


def cross_kernel(
    lists, received, earlier_rows, earlier, first, first_radii, out,
    second, second_radii, rows, columns, listed, sem,
):
    copy = pltpu.make_async_copy(lists, listed, sem)
    copy.start()
    rows[...] = earlier_rows[...]
    columns[...] = jnp.zeros_like(columns)
    for rank in range(RANKS):
        prepare_second(second, second_radii, received, rank)
    copy.wait()
    credit_list(first, first_radii, second, second_radii, rows, columns, listed, 1)
    factor = 1.0 / (TIMES * BLOCK)
    own = (earlier[...] + rows[...].T[0:BLOCKS, :]) * factor
    beyond = block_sums(columns) * factor
    for block in range(BLOCKS):
        rank, half = divmod(block, 2)
        for k in range(2):
            at = 2 * half + k
            out[rank, at : at + 1, :] = own[block : block + 1, k * 128 : (k + 1) * 128]
            out[rank, 4 + at : 5 + at, :] = beyond[block : block + 1, k * 128 : (k + 1) * 128]


def body(coefs, radii, pair_blocks, pair_count):
    in_vmem = pl.BlockSpec(memory_space=VMEM)
    table = jnp.asarray(spread_table())
    coefs = coefs.transpose(1, 0, 2)
    at_all = pl.pallas_call(
        evaluate_kernel,
        out_shape=jax.ShapeDtypeStruct((RANKS, CHUNK, 128), F32),
        in_specs=[pl.BlockSpec(memory_space=SMEM)] + [pl.BlockSpec(memory_space=pltpu.HBM)] * 4,
        out_specs=in_vmem,
        scratch_shapes=[
            SMEM(pair_blocks.shape, jnp.int32),
            VMEM(table.shape, BF16),
            VMEM(coefs.shape, F32),
            VMEM(radii.shape, F32),
            pltpu.SemaphoreType.DMA((4,)),
        ],
        compiler_params=PARAMS,
        name="evaluate",
    )(pair_count, *(pltpu.with_memory_space_constraint(x, pltpu.HBM) for x in (pair_blocks, table, coefs, radii)))
    received = lax.all_to_all(at_all, "rank", 0, 0)
    beyond = passed_along(received, "shell", -1)
    rows, credited, first, first_radii, lists = pl.pallas_call(
        own_kernel,
        out_shape=[
            jax.ShapeDtypeStruct((BLOCK, 128), F32),
            jax.ShapeDtypeStruct((BLOCKS, BLOCK), F32),
            jax.ShapeDtypeStruct((SPAN, 128), BF16),
            jax.ShapeDtypeStruct((SPAN, 128), F32),
            jax.ShapeDtypeStruct((2, LISTS), jnp.int32),
        ],
        in_specs=[in_vmem],
        out_specs=[in_vmem] * 5,
        scratch_shapes=[
            VMEM((128, SPAN), BF16),
            VMEM((BLOCKS, BLOCK), F32),
            VMEM((8 * BLOCKS + 8, BLOCK), F32),
            SMEM((2, LISTS), jnp.int32),
            pltpu.SemaphoreType.DMA,
        ],
        compiler_params=PARAMS,
        cost_estimate=pl.CostEstimate(flops=8_000_000_000, bytes_accessed=8_000_000, transcendentals=0),
        name="own_pairs",
    )(received)
    partial = pl.pallas_call(
        cross_kernel,
        out_shape=jax.ShapeDtypeStruct((RANKS, 8, 128), F32),
        in_specs=[in_vmem] * 6,
        out_specs=in_vmem,
        scratch_shapes=[
            VMEM((128, SPAN), BF16),
            VMEM((BLOCKS, BLOCK), F32),
            VMEM((BLOCK, 128), F32),
            VMEM((8 * BLOCKS + 8, BLOCK), F32),
            SMEM((2, LISTS), jnp.int32),
            pltpu.SemaphoreType.DMA,
        ],
        compiler_params=PARAMS,
        cost_estimate=pl.CostEstimate(flops=8_000_000_000, bytes_accessed=8_000_000, transcendentals=0),
        name="crossing_pairs",
    )(lists, beyond, rows, credited, first, first_radii)
    summed = jnp.sum(lax.all_to_all(partial, "rank", 0, 0), axis=0)
    returned = passed_along(summed[4:], "shell", 1)
    return (summed[:4] + returned).reshape(HELD)


def solution(mesh):
    placed = (
        P(None, None, ("shell", "rank")),
        P(("shell", "rank")),
        P(None, ("shell", "rank")),
        P(("shell", "rank")),
    )
    return jax.shard_map(
        body, mesh=mesh, in_specs=placed, out_specs=P(("shell", "rank")), check_vma=False
    )
```

```python
import jax
import jax.numpy as jnp
import ml_dtypes
import numpy as np
from jax import lax
from jax.experimental import pallas as pl
from jax.experimental.pallas import tpu as pltpu
from jax.sharding import PartitionSpec as P

NCOEF = 16
TIMES = 64
BLOCK = 256
RANKS = 16
SLOTS = 8
BLOCKS = 32
SPAN = BLOCKS * BLOCK
HELD = 512
STEPS = (24, 8, 4)
LIST = 160
LISTS = 512
COUNTS = 480
TILE = 64
F32 = jnp.float32
BF16 = jnp.bfloat16
VMEM = pltpu.VMEM
SMEM = pltpu.SMEM
PARAMS = pltpu.CompilerParams(vmem_limit_bytes=24 * 1024 * 1024)


def passed_along(value, axis, steps):
    count = lax.axis_size(axis)
    leading, last = (max(0, -steps), min(count, count - steps))
    return lax.ppermute(value, axis, [(source, source + steps) for source in range(leading, last)])


EIGHT = ((0, 0), (0, 1), (0, 2), (3, 0), (1, 0), (1, 1), (1, 2), (3, 1))
FOUR = ((2, 0), (2, 1), (2, 2), (3, 2))
CHUNK = 56


def spread_table():
    node = -1.0 + (2.0 * np.arange(TIMES) + 1.0) / TIMES
    table = np.cos(np.arange(NCOEF)[None, :] * np.arccos(node)[:, None])
    spread = np.zeros((RANKS, 16, 3, NCOEF), np.float32)
    for row, (time, coordinate) in enumerate(EIGHT + FOUR + FOUR):
        spread[:, row, coordinate, :] = table[time :: TIMES // RANKS]
    spread = spread.reshape(RANKS * 16, 3 * NCOEF)
    high = spread.astype(ml_dtypes.bfloat16)
    mid = (spread - high.astype(np.float32)).astype(ml_dtypes.bfloat16)
    low = (spread - high.astype(np.float32) - mid.astype(np.float32)).astype(ml_dtypes.bfloat16)
    return np.stack([np.concatenate([high, mid], axis=1), np.concatenate([high, low], axis=1)])


def evaluate_kernel(*refs):
    count, *given = refs[:5]
    out, *held, sems = refs[5:]
    copies = [pltpu.make_async_copy(given[i], held[i], sems.at[i]) for i in range(4)]
    pairs, table, coefs, radii = held
    for i in (2, 1, 0, 3):
        copies[i].start()
    copies[2].wait()
    high, mid, low = pieces(coefs[...].reshape(3 * NCOEF, HELD))
    for i in (1, 0, 3):
        copies[i].wait()
    values = None
    for which, above, below in ((0, high, high), (0, mid, mid), (1, low, high)):
        part = jnp.dot(table[which], jnp.concatenate([above, below], axis=0), preferred_element_type=F32)
        values = part if values is None else values + part
    values = values.reshape(RANKS, 16, HELD)
    lane = lax.broadcasted_iota(jnp.int32, (1, 128), 1)
    row = lax.broadcasted_iota(jnp.int32, (8, 128), 0)
    last = jnp.where(row == 6, count[0].astype(F32), 0.0)
    for q in range(4):
        last = jnp.where(row == q, radii[128 * q : 128 * q + 128].reshape(1, 128), last)
    for side in range(2):
        blocks = jnp.zeros((1, 128), F32)
        for slot in range(SLOTS):
            blocks = jnp.where(lane == slot, pairs[side, slot].astype(F32), blocks)
        last = jnp.where(row == 4 + side, blocks, last)
    runs = [values[:, :, 128 * q : 128 * q + 128] for q in range(4)]
    for q in range(4):
        out[:, 8 * q : 8 * q + 8, :] = runs[q][:, 0:8]
    for half in range(2):
        out[:, 32 + 8 * half : 40 + 8 * half, :] = jnp.where(
            row[None] < 4, runs[2 * half][:, 8:16], runs[2 * half + 1][:, 8:16]
        )
    out[:, 48:56, :] = jnp.broadcast_to(last[None], (RANKS, 8, 128))


def list_pairs(received):
    first, second, count = (received[:, row, 0:128] for row in (52, 53, 54))
    lane = lax.broadcasted_iota(jnp.int32, (RANKS, 128), 1)
    live = (lane < SLOTS) & (lane.astype(F32) < count)
    before_lane = jnp.where(
        lax.broadcasted_iota(jnp.int32, (128, 128), 0) < lax.broadcasted_iota(jnp.int32, (128, 128), 1), 1.0, 0.0
    ).astype(BF16)
    before_rank = jnp.where(
        lax.broadcasted_iota(jnp.int32, (RANKS, RANKS), 1) < lax.broadcasted_iota(jnp.int32, (RANKS, RANKS), 0), 1.0, 0.0
    ).astype(BF16)
    ones = jnp.ones((128, 128), BF16)
    crosses = second >= BLOCKS
    place = jnp.full((RANKS, 128), -1.0, F32)
    totals = []
    for which, chosen in enumerate((live & ~crosses, live & crosses)):
        flag = jnp.where(chosen, 1.0, 0.0).astype(BF16)
        within = jnp.dot(flag, before_lane, preferred_element_type=F32)
        ranks = jnp.dot(before_rank, flag, preferred_element_type=F32).astype(BF16)
        position = within + jnp.dot(ranks, ones, preferred_element_type=F32)
        place = jnp.where(chosen, position + which * LIST, place)
        totals.append(jnp.sum(flag.astype(F32), keepdims=True))
    second = jnp.where(crosses, second - BLOCKS, second)
    target = lax.broadcasted_iota(jnp.int32, (RANKS, LISTS), 1).astype(F32)
    sides = [jnp.zeros((RANKS, LISTS), F32)] * 2
    for slot in range(SLOTS):
        hit = place[:, slot : slot + 1] == target
        sides = [
            kept + jnp.where(hit, side[:, slot : slot + 1] - BLOCKS, 0.0) for kept, side in zip(sides, (first, second))
        ]
    lists = jnp.concatenate([jnp.sum(side, axis=0, keepdims=True) for side in sides], axis=0) + BLOCKS
    for which, total in enumerate(totals):
        lists = jnp.where(target[0:2] == COUNTS + which, total, lists)
    return lists.astype(jnp.int32)


def pieces(x):
    high = x.astype(BF16)
    rest = x - high.astype(F32)
    mid = rest.astype(BF16)
    low = (rest - mid.astype(F32)).astype(BF16)
    return high, mid, low


def radii_of(received, rank):
    return jnp.concatenate([received[rank, 48 + q : 49 + q, :] for q in range(4)], axis=1)


def features(received, rank):
    n = HELD
    radii = radii_of(received, rank)
    row = lax.broadcasted_iota(jnp.int32, (8, n), 0)
    eight = jnp.concatenate([received[rank, 8 * q : 8 * q + 8, :] for q in range(4)], axis=1)
    four = []
    for half in range(2):
        both = received[rank, 32 + 8 * half : 40 + 8 * half, :]
        four += [both, pltpu.roll(both, 4, 0)]
    four = jnp.concatenate(four, axis=1)
    upper = jnp.where(row % 4 == 3, radii, eight)
    lower = jnp.where(row < 3, four, radii)
    for at, moved in ((4, pltpu.roll(eight, 1, 0)), (5, pltpu.roll(eight, 6, 0)), (6, pltpu.roll(four, 3, 0))):
        lower = jnp.where(row == at, moved, lower)
    part = lax.broadcasted_iota(jnp.int32, (16, n), 0) % 4
    values = jnp.concatenate([upper, lower], axis=0)
    square = (values * values).reshape(2, 8, n)
    row = lax.broadcasted_iota(jnp.int32, (2, 8, n), 1)
    twos = square + jnp.where(row % 2 == 1, pltpu.roll(square, 1, 1), pltpu.roll(square, 7, 1))
    fours = twos + jnp.where((row // 2) % 2 == 1, pltpu.roll(twos, 2, 1), pltpu.roll(twos, 6, 1))
    high, mid, low = pieces(values)
    s_high, s_mid, s_low = (p.astype(F32) for p in pieces(fours.reshape(16, n)))
    zero = jnp.zeros((16, n), F32)
    sums = jnp.where(part == 0, s_high, jnp.where(part == 1, s_mid, jnp.where(part == 2, s_low, zero)))
    ones = jnp.where(part == 3, zero, 1.0)
    return high, mid, low, sums, ones, part


def prepare_second(second, second_radii, received, rank):
    high, mid, low, sums, ones, _ = features(received, rank)
    radii = radii_of(received, rank)
    terms = (high, mid, high, low, high, mid, sums.astype(BF16), ones.astype(BF16))
    for i, term in enumerate(terms):
        second[16 * i : 16 * i + 16, rank * HELD : (rank + 1) * HELD] = term
    for half in range(HELD // BLOCK):
        block = rank * (HELD // BLOCK) + half
        second_radii[block : block + 1, :] = radii[:, half * BLOCK : (half + 1) * BLOCK]


def prepare_first(first, first_radii, received, rank):
    high, mid, low, sums, ones, part = features(received, rank)
    radii = radii_of(received, rank)
    scale = jnp.where(part == 3, 2.0, -2.0)
    high, mid, low = (scale * p.astype(F32) for p in (high, mid, low))
    terms = jnp.concatenate([high, high, mid, high, low, mid, ones, sums], axis=0)
    for c in range(0, HELD, 128):
        at = rank * HELD + c
        first[at : at + 128, :] = terms[:, c : c + 128].T.astype(BF16)
        first_radii[at : at + 128, :] = jnp.broadcast_to(radii[:, c : c + 128], (128, 128)).T


def credit_pair(first, first_radii, second, second_radii, rows, columns, a, b):
    from_a = pl.multiple_of(lax.rem(a, BLOCKS) * BLOCK, BLOCK)
    block_b = lax.rem(b, BLOCKS)
    of_b = second[:, pl.ds(pl.multiple_of(block_b * BLOCK, BLOCK), BLOCK)]
    radii_b = second_radii[pl.ds(block_b, 1), :]
    lane = lax.broadcasted_iota(jnp.int32, (TILE, 128), 1)
    masks = [jnp.where((lane % 16) // 4 == t, 1.0, 0.0).astype(BF16) for t in range(4)]
    column = jnp.zeros((8, BLOCK), F32)
    for i in range(0, BLOCK, TILE):
        of_a = first[pl.ds(from_a + i, TILE), :]
        total = None
        for mask in masks:
            whole = jnp.dot(of_a * mask, of_b, preferred_element_type=F32)
            inverse = pl.reciprocal(whole, approx=False)
            total = inverse if total is None else total + inverse
        radii_a = first_radii[pl.ds(from_a + i, TILE), :]
        summed = jnp.concatenate([radii_a, radii_a], axis=1) + radii_b
        weight = total * (summed * summed)
        column = column + jnp.sum(weight.reshape(TILE // 8, 8, BLOCK), axis=0)
        row = jnp.sum(weight[:, :128] + weight[:, 128:], axis=1, keepdims=True)
        rows[i : i + TILE, :] = rows[i : i + TILE, :] + jnp.where(lane == a, row, 0.0)
    at = pl.ds(pl.multiple_of(b * 8, 8), 8)
    columns[at, :] = columns[at, :] + column


def credit_list(first, first_radii, second, second_radii, rows, columns, lists, which):
    count = lists[0, COUNTS + which]
    done = jnp.int32(0)
    for pairs in STEPS:
        steps = jnp.maximum(count - done + 3, 0) // pairs

        @pl.loop(0, steps)
        def _(step):
            for u in range(pairs):
                at = which * LIST + done + step * pairs + u
                credit_pair(first, first_radii, second, second_radii, rows, columns, lists[0, at], lists[1, at])

        done = done + steps * pairs


def block_sums(columns):
    return jnp.sum(columns[0 : 8 * BLOCKS, :].reshape(BLOCKS, 8, BLOCK), axis=1)


def own_kernel(
    received, rows, credited, first, first_radii, lists,
    second, second_radii, columns, listed, sem,
):
    lists[...] = list_pairs(received)
    copy = pltpu.make_async_copy(lists, listed, sem)
    copy.start()
    rows[...] = jnp.zeros_like(rows)
    columns[...] = jnp.zeros_like(columns)
    for rank in range(RANKS):
        prepare_second(second, second_radii, received, rank)
        prepare_first(first, first_radii, received, rank)
    copy.wait()
    credit_list(first, first_radii, second, second_radii, rows, columns, listed, 0)
    credited[...] = block_sums(columns)


def cross_kernel(
    lists, received, earlier_rows, earlier, first, first_radii, out,
    second, second_radii, rows, columns, listed, sem,
):
    copy = pltpu.make_async_copy(lists, listed, sem)
    copy.start()
    rows[...] = earlier_rows[...]
    columns[...] = jnp.zeros_like(columns)
    for rank in range(RANKS):
        prepare_second(second, second_radii, received, rank)
    copy.wait()
    credit_list(first, first_radii, second, second_radii, rows, columns, listed, 1)
    factor = 1.0 / (TIMES * BLOCK)
    own = (earlier[...] + rows[...].T[0:BLOCKS, :]) * factor
    beyond = block_sums(columns) * factor
    for block in range(BLOCKS):
        rank, half = divmod(block, 2)
        for k in range(2):
            at = 2 * half + k
            out[rank, at : at + 1, :] = own[block : block + 1, k * 128 : (k + 1) * 128]
            out[rank, 4 + at : 5 + at, :] = beyond[block : block + 1, k * 128 : (k + 1) * 128]


def body(coefs, radii, pair_blocks, pair_count):
    in_vmem = pl.BlockSpec(memory_space=VMEM)
    table = jnp.asarray(spread_table())
    coefs = coefs.transpose(1, 0, 2)
    at_all = pl.pallas_call(
        evaluate_kernel,
        out_shape=jax.ShapeDtypeStruct((RANKS, CHUNK, 128), F32),
        in_specs=[pl.BlockSpec(memory_space=SMEM)] + [pl.BlockSpec(memory_space=pltpu.HBM)] * 4,
        out_specs=in_vmem,
        scratch_shapes=[
            SMEM(pair_blocks.shape, jnp.int32),
            VMEM(table.shape, BF16),
            VMEM(coefs.shape, F32),
            VMEM(radii.shape, F32),
            pltpu.SemaphoreType.DMA((4,)),
        ],
        compiler_params=PARAMS,
        name="evaluate",
    )(pair_count, *(pltpu.with_memory_space_constraint(x, pltpu.HBM) for x in (pair_blocks, table, coefs, radii)))
    received = lax.all_to_all(at_all, "rank", 0, 0)
    beyond = passed_along(received, "shell", -1)
    rows, credited, first, first_radii, lists = pl.pallas_call(
        own_kernel,
        out_shape=[
            jax.ShapeDtypeStruct((BLOCK, 128), F32),
            jax.ShapeDtypeStruct((BLOCKS, BLOCK), F32),
            jax.ShapeDtypeStruct((SPAN, 128), BF16),
            jax.ShapeDtypeStruct((SPAN, 128), F32),
            jax.ShapeDtypeStruct((2, LISTS), jnp.int32),
        ],
        in_specs=[in_vmem],
        out_specs=[in_vmem] * 5,
        scratch_shapes=[
            VMEM((128, SPAN), BF16),
            VMEM((BLOCKS, BLOCK), F32),
            VMEM((8 * BLOCKS + 8, BLOCK), F32),
            SMEM((2, LISTS), jnp.int32),
            pltpu.SemaphoreType.DMA,
        ],
        compiler_params=PARAMS,
        cost_estimate=pl.CostEstimate(flops=8_000_000_000, bytes_accessed=8_000_000, transcendentals=0),
        name="own_pairs",
    )(received)
    partial = pl.pallas_call(
        cross_kernel,
        out_shape=jax.ShapeDtypeStruct((RANKS, 8, 128), F32),
        in_specs=[in_vmem] * 6,
        out_specs=in_vmem,
        scratch_shapes=[
            VMEM((128, SPAN), BF16),
            VMEM((BLOCKS, BLOCK), F32),
            VMEM((BLOCK, 128), F32),
            VMEM((8 * BLOCKS + 8, BLOCK), F32),
            SMEM((2, LISTS), jnp.int32),
            pltpu.SemaphoreType.DMA,
        ],
        compiler_params=PARAMS,
        cost_estimate=pl.CostEstimate(flops=8_000_000_000, bytes_accessed=8_000_000, transcendentals=0),
        name="crossing_pairs",
    )(lists, beyond, rows, credited, first, first_radii)
    summed = jnp.sum(lax.all_to_all(partial, "rank", 0, 0), axis=0)
    returned = passed_along(summed[4:], "shell", 1)
    return (summed[:4] + returned).reshape(HELD)


def solution(mesh):
    placed = (
        P(None, None, ("shell", "rank")),
        P(("shell", "rank")),
        P(None, ("shell", "rank")),
        P(("shell", "rank")),
    )
    return jax.shard_map(
        body, mesh=mesh, in_specs=placed, out_specs=P(("shell", "rank")), check_vma=False
    )
```
